128 devices in a mesh: wide: 64 (over x, y, z), narrow: 2 (over core).
Axes of the slice: x: 4, y: 4, z: 4, core: 2. Of those that a mesh axis runs over, the one named last changes fastest.
Arguments:
- user_emb: float32 [256, 512, 256], P('wide'), may hold values from -0.75 to 0.75
- item_emb: float32 [128, 512, 256], P('wide', 'narrow'), may hold values from -0.75 to 0.75
- pairs: int32 [64, 64, 3], P('wide'), may hold values from 0 to 255, as said below
- counts: int32 [64], P('wide'), may hold values from 57 to 64
- natural_exponent_param: float32 [1], replicated, may hold values from 1.5 to 2.5
- additive_shift_param: float32 [1], replicated, may hold values from -3 to -1
Outputs:
- user_grad: float32 [256, 512, 256], P('wide')
- item_grad: float32 [128, 512, 256], P('wide', 'narrow')
- objective_summary_vector: float32 [3], replicated
The draws below stay inside these ranges and needn't reach their ends.
Inputs may be any that keep to these rules, and one draw needn't show every extreme that they name: `pairs`: row w lists slots (user block, item block, label): the user block lies in w * 4 to (w + 1) * 4 - 1; over the 64 slots of one row, item block // 2 takes every value 0 to 63 exactly once; label 1 is a positive pair, 0 a hard negative; slots at or past counts[w] are ignored.
All inputs are finite; a program needn't handle non-finite values.
Results may differ from the reference program's by a relative error of at most 0.0032.
Values may be sent and summed in bfloat16 or wider, within the bound.
No kernel may reach another device: no remote copies, remote signals or barrier semaphores. Data moves between devices by JAX's collectives and lax.ppermute only.
A program may use at most 128 MiB of HBM per device.

```python
import jax
import jax.numpy as jnp
from jax import lax

E = 256
TILE_HEIGHT = 512
UB = 4
IB = 2
P_MAX = 64
UBLOCKS = 256
IBLOCKS = 128
N_NARROW = 2


def draw_pairs(key, part):
    key = jax.random.fold_in(key, 5)
    wide_count = UBLOCKS // UB
    row_keys = jax.random.split(key, wide_count)

    def one_row(row_key, row_index):
        key_owner, key_item, key_user, key_label = jax.random.split(row_key, 4)
        owners = jax.random.permutation(key_owner, wide_count)[:P_MAX]
        item_ids = owners * IB + jax.random.randint(key_item, (P_MAX,), 0, IB)
        user_ids = row_index * UB + jax.random.randint(key_user, (P_MAX,), 0, UB)
        pair_labels = jax.random.randint(key_label, (P_MAX,), 0, 2)
        return jnp.stack([user_ids, item_ids, pair_labels], axis=1)
    return jax.vmap(one_row)(row_keys, jnp.arange(wide_count)).astype(jnp.int32)


def draw_counts(key, part):
    key = jax.random.fold_in(key, 9)
    wide_count = UBLOCKS // UB
    key_short, key_full = jax.random.split(key, 2)
    shortfall = jax.random.randint(key_short, (wide_count,), 0, P_MAX // 8)
    full_row = jax.random.randint(key_full, (), 0, wide_count)
    return jnp.where(jnp.arange(wide_count) == full_row, P_MAX, P_MAX - shortfall).astype(jnp.int32)


def shard_levels(rng, extent, cuts, low, largest):
    level, own = 1.0, jax.random.fold_in(rng, 6)
    for position, parts in cuts:
        draws = jnp.exp(jax.random.uniform(jax.random.fold_in(own, position), (parts,), jnp.float32, low / len(cuts), largest / len(cuts)))
        level = level * jnp.repeat(draws, extent[position] // parts).reshape([-1 if axis == position else 1 for axis in range(len(extent))])
    return level


def bell_draw(rng, extent, spread, most, cuts=(), held_as=jnp.bfloat16):
    drawn = spread * jax.random.normal(rng, extent, jnp.float32)
    if cuts:
        drawn = drawn * shard_levels(rng, extent, cuts, -0.22, 0.18)
    return jnp.clip(drawn, -most, most).astype(held_as)


def setup_inputs(seed: int = 0) -> dict:
    arg_keys = jax.random.split(jax.random.key(seed), 7)
    return {
        "user_emb": bell_draw(arg_keys[0], (UBLOCKS, TILE_HEIGHT, E), 0.125, 0.75, ((0, 64),), jnp.float32),
        "item_emb": bell_draw(arg_keys[1], (IBLOCKS, TILE_HEIGHT, E), 0.125, 0.75, ((0, 64), (1, 2)), jnp.float32),
        "pairs": draw_pairs(jax.random.fold_in(arg_keys[6], 71), 0),
        "counts": draw_counts(jax.random.fold_in(arg_keys[6], 71), 0),
        "natural_exponent_param": jnp.clip(jax.random.uniform(arg_keys[4], (1,), jnp.float32, 1.5, 2.5), 1.5, 2.5),
        "additive_shift_param": jnp.clip(jax.random.uniform(arg_keys[5], (1,), jnp.float32, -3.0, -1.0), -3.0, -1.0),
    }


def reference(user_emb, item_emb, pairs, counts, natural_exponent_param, additive_shift_param):
    user_b = user_emb.astype(jnp.bfloat16)
    item_b = item_emb.astype(jnp.bfloat16)
    slot_count = pairs.shape[1]
    flat_pairs = pairs.reshape(-1, 3)
    alive = (jnp.arange(slot_count)[None, :] < counts[:, None]).reshape(-1)
    sharpness_multiplier = jnp.exp(natural_exponent_param[0])
    logistic_weight = sharpness_multiplier * (TILE_HEIGHT ** -0.5)
    half_rows = TILE_HEIGHT // N_NARROW
    row_ids = jnp.arange(TILE_HEIGHT)[:, None]
    col_ids = jnp.arange(TILE_HEIGHT)[None, :]
    diagonal_flag = row_ids == col_ids

    def work(state_now, pair_row):
        user_acc, item_acc, objective_accum, multiplier_derivative_accum, shift_derivative_accum = state_now
        user_tile = lax.dynamic_index_in_dim(user_b, pair_row[0], 0, keepdims=False)
        item_tile = lax.dynamic_index_in_dim(item_b, pair_row[1], 0, keepdims=False)
        similarity_dot = lax.dot_general(user_tile, item_tile, (((1,), (1,)), ((), ())), preferred_element_type=jnp.float32)
        couple_affinities = sharpness_multiplier * similarity_dot + additive_shift_param[0]
        target = jnp.where((pair_row[2] == 1) & diagonal_flag, 1.0, -1.0).astype(similarity_dot.dtype)
        margin = -target * couple_affinities
        objective_accum = objective_accum + jnp.sum(jax.nn.softplus(margin))
        weight = -target * jax.nn.sigmoid(margin)
        multiplier_derivative_accum = multiplier_derivative_accum + jnp.sum(weight * similarity_dot)
        shift_derivative_accum = shift_derivative_accum + jnp.sum(weight)
        scaled = (weight * logistic_weight).astype(jnp.bfloat16)
        split_scaled = scaled.reshape(TILE_HEIGHT, N_NARROW, half_rows).astype(jnp.float32)
        split_item = item_tile.reshape(N_NARROW, half_rows, item_tile.shape[1]).astype(jnp.float32)
        user_parts = jnp.einsum("rhc,hce->hre", split_scaled, split_item)
        user_parts = lax.optimization_barrier(user_parts.astype(jnp.bfloat16)).astype(user_acc.dtype)
        user_part = jnp.sum(user_parts, axis=0)
        old_user = lax.dynamic_index_in_dim(user_acc, pair_row[0], 0, keepdims=False)
        user_acc = lax.dynamic_update_index_in_dim(user_acc, old_user + user_part, pair_row[0], 0)
        item_part = lax.dot_general(scaled, user_tile, (((0,), (0,)), ((), ())), preferred_element_type=jnp.float32)
        item_part = lax.optimization_barrier(item_part.astype(jnp.bfloat16)).astype(item_acc.dtype)
        old_item = lax.dynamic_index_in_dim(item_acc, pair_row[1], 0, keepdims=False)
        item_acc = lax.dynamic_update_index_in_dim(item_acc, old_item + item_part, pair_row[1], 0)
        return (user_acc, item_acc, objective_accum, multiplier_derivative_accum, shift_derivative_accum)

    def visit_pair(state_now, entry):
        pair_row, live_flag = entry
        state_next = lax.cond(live_flag, work, lambda given, unused: given, state_now, pair_row)
        return state_next, None

    zero = jnp.zeros((), jnp.float32)
    initial = (jnp.zeros(user_emb.shape, jnp.float32), jnp.zeros(item_emb.shape, jnp.float32), zero, zero, zero)
    final_state, unused = lax.scan(visit_pair, initial, (flat_pairs, alive))
    user_grad, item_grad, objective_accum, multiplier_derivative_accum, shift_derivative_accum = final_state
    couple_normalizer = TILE_HEIGHT * TILE_HEIGHT * jnp.sum(counts).astype(jnp.float32)
    objective_summary_vector = jnp.stack([objective_accum / couple_normalizer, sharpness_multiplier * multiplier_derivative_accum / couple_normalizer, shift_derivative_accum / couple_normalizer])
    return user_grad, item_grad, objective_summary_vector
```

```python
import functools

import jax
import jax.numpy as jnp
from jax import lax
from jax.experimental import pallas as pl
from jax.experimental.pallas import tpu as pltpu
from jax.sharding import Mesh
from jax.sharding import PartitionSpec as P

LOG2E = 1.4426950408889634
RING = 4
NT = (((1,), (1,)), ((), ()))
NN = (((1,), (0,)), ((), ()))
TN = (((0,), (0,)), ((), ()))
WIDE = ("x", "y", "z")
BF = jnp.bfloat16
F32 = jnp.float32


def score_kernel(
    place, table, scalars, own_users, near_users, far_users, items_in,
    user_keep, user_give, item_keep, item_give, sums,
    users, items, uacc, iacc, ugive, igive, eye, jobs, in_sem, out_sem,
):
    my_x, my_y, my_z, core = place[0], place[1], place[2], place[3]
    blocks, height, width = own_users.shape
    half = height // 2
    mine = pl.multiple_of(core * half, half)
    other = pl.multiple_of((1 - core) * half, half)
    copies = [
        pltpu.make_async_copy(items_in, items, in_sem.at[0]),
        pltpu.make_async_copy(own_users, users.at[pl.ds(0, blocks)], in_sem.at[1]),
    ]
    for d in range(1, RING):
        rows = pl.ds(d * blocks, blocks)
        copies.append(pltpu.make_async_copy(
            near_users.at[pl.ds((d - 1) * blocks, blocks)],
            users.at[rows, pl.ds(mine, half), :], in_sem.at[2 * d]))
        copies.append(pltpu.make_async_copy(
            far_users.at[pl.ds((d - 1) * blocks, blocks)],
            users.at[rows, pl.ds(other, half), :], in_sem.at[2 * d + 1]))
    for c in copies:
        c.start()

    slots = 64

    def list_slot(i, count):
        d = i // slots
        slot = i % slots
        user, item, label = table[i * 3], table[i * 3 + 1], table[i * 3 + 2]
        owner = item // 2
        dx = (my_x - owner // 16) & 3
        dy = (my_y - (owner // 4) % 4) & 3
        first = jnp.where(core == 0, dy, dx)
        second = jnp.where(core == 0, dx, dy)
        jobs[count] = d * blocks + (user & (blocks - 1))
        jobs[count + 72] = (second * RING + first) * 2 + (item & 1)
        jobs[count + 144] = label
        live = (owner % 4 == my_z) & (slot < table[RING * slots * 3 + d])
        return count + live.astype(jnp.int32)

    count = lax.fori_loop(0, RING * slots, list_slot, jnp.int32(0), unroll=4)
    jobs[count] = 0
    jobs[count + 72] = 0
    jobs[count + 144] = 0

    uacc[...] = jnp.zeros_like(uacc)
    iacc[...] = jnp.zeros_like(iacc)
    row = lax.broadcasted_iota(jnp.int32, (128, 128), 0)
    col = lax.broadcasted_iota(jnp.int32, (128, 128), 1)
    eye[...] = (row == col).astype(F32)
    for c in copies:
        c.wait()

    slope, shift, gain = scalars[0], scalars[1], scalars[2]

    def tile(u, it, slope_j, shift_j, label_j):
        inner = lax.dot_general(u, it, NT, preferred_element_type=F32)
        x = inner * slope_j + shift_j
        e = jnp.exp2(-jnp.abs(x))
        t = 1.0 + e
        high = x >= 0.0
        num = jnp.where(high, 1.0, e)
        soft = jnp.maximum(x, 0.0)
        if label_j is not None:
            hit = eye[...] * label_j > 0.5
            nums, softs = [], []
            for q in range(2):
                r = slice(q * 128, (q + 1) * 128)
                xb, eb = x[r, r], e[r, r]
                nb = jnp.where(hit, jnp.where(high[r, r], -eb, -1.0), num[r, r])
                sb = soft[r, r] - jnp.where(hit, xb, 0.0)
                keep = slice((1 - q) * 128, (2 - q) * 128)
                nums.append(jnp.concatenate([nb, num[r, keep]] if q == 0 else [num[r, keep], nb], axis=1))
                softs.append(jnp.concatenate([sb, soft[r, keep]] if q == 0 else [soft[r, keep], sb], axis=1))
            num = jnp.concatenate(nums, axis=0)
            soft = jnp.concatenate(softs, axis=0)
        w = num * pl.reciprocal(t, approx=True)
        scaled = (w * gain).astype(BF)
        tt = t.reshape(8, 32, 256)
        ee = e.reshape(8, 32, 256)
        prod = ee[0]
        for m in range(1, 8):
            prod = prod * tt[m] + ee[m]
        pr = prod.reshape(4, 8, 256)
        p0 = pr[0] + pr[1] + pr[0] * pr[1]
        p1 = pr[2] + pr[3] + pr[2] * pr[3]
        p = p0 + p1 + p0 * p1
        logs = jnp.where(p < 1e-3, p * (1.0 - 0.5 * p), jnp.log(1.0 + p))
        soft_sum = soft.reshape(32, 8, 256).sum(0)
        w_sum = w.reshape(32, 8, 256).sum(0)
        return scaled, soft_sum, logs, w_sum

    def one_job(j, valid, carry):
        soft_acc, log_acc, w_acc = carry
        ui, ii = jobs[j], jobs[j + 72]
        label_j = jobs[j + 144].astype(F32)
        slope_j = jnp.where(valid, slope, 0.0)
        shift_j = jnp.where(valid, shift, -1e30)
        label_j = jnp.where(valid, label_j, 0.0)
        it = items[ii]
        um = users[ui, pl.ds(mine, half), :]
        uo = users[ui, pl.ds(other, half), :]
        sm, a0, l0, w0 = tile(um, it, slope_j, shift_j, label_j)
        so, a1, l1, w1 = tile(uo, it, slope_j, shift_j, None)
        uacc[ui, pl.ds(mine, half), :] += lax.dot_general(sm, it, NN, preferred_element_type=F32)
        uacc[ui, pl.ds(other, half), :] += lax.dot_general(so, it, NN, preferred_element_type=F32)
        iacc[ii] += (lax.dot_general(sm, um, TN, preferred_element_type=F32)
                     + lax.dot_general(so, uo, TN, preferred_element_type=F32))
        return soft_acc + (a0 + a1), log_acc + (l0 + l1), w_acc + (w0 + w1)

    def two_jobs(g, carry):
        carry = one_job(2 * g, True, carry)
        return one_job(2 * g + 1, 2 * g + 1 < count, carry)

    zero = jnp.zeros((8, 256), F32)
    soft_acc, log_acc, w_acc = lax.fori_loop(0, (count + 1) // 2, two_jobs, (zero, zero, zero))

    sends = RING * 2
    out = [
        pltpu.make_async_copy(uacc.at[:, pl.ds(mine, half), :], user_keep, out_sem.at[0]),
        pltpu.make_async_copy(iacc.at[pl.ds(0, sends)], item_keep, out_sem.at[1]),
    ]
    for c in out:
        c.start()

    def user_out(b, acc):
        given = uacc[b, pl.ds(other, half), :]
        ugive[b] = given.astype(BF)
        kept = uacc[b, pl.ds(mine, half), :]
        prod = (kept * users[b, pl.ds(mine, half), :].astype(F32)
                + given * users[b, pl.ds(other, half), :].astype(F32))
        return acc + prod.reshape(32, 8, 256).sum(0)

    scale_acc = lax.fori_loop(0, RING * blocks, user_out, zero)
    c = pltpu.make_async_copy(ugive, user_give, out_sem.at[2])
    c.start()
    out.append(c)

    def item_out(b, none):
        igive[b] = iacc[b + sends].astype(BF)
        return none

    lax.fori_loop(0, (RING - 1) * sends, item_out, 0)
    c = pltpu.make_async_copy(igive, item_give, out_sem.at[3])
    c.start()
    out.append(c)
    sums[0] = soft_acc * (1.0 / LOG2E) + log_acc
    sums[1] = scale_acc * scalars[3]
    sums[2] = w_acc
    for c in out:
        c.wait()


def score(place, table, scalars, own_users, near_users, far_users, items_in):
    blocks, height, width = own_users.shape
    half = height // 2
    n_users, n_items = RING * blocks, items_in.shape[0]
    smem = pl.BlockSpec(memory_space=pltpu.SMEM)
    any_ = pl.BlockSpec(memory_space=pl.ANY)
    return pl.pallas_call(
        score_kernel,
        in_specs=[smem, smem, smem, any_, any_, any_, any_],
        out_specs=[any_, any_, any_, any_, pl.BlockSpec(memory_space=pltpu.VMEM)],
        out_shape=[
            jax.ShapeDtypeStruct((n_users, half, width), F32),
            jax.ShapeDtypeStruct((n_users, half, width), BF),
            jax.ShapeDtypeStruct((2 * RING, half, width), F32),
            jax.ShapeDtypeStruct((n_items - 2 * RING, half, width), BF),
            jax.ShapeDtypeStruct((3, 8, width), F32),
        ],
        scratch_shapes=[
            pltpu.VMEM((n_users, height, width), BF),
            pltpu.VMEM((n_items, half, width), BF),
            pltpu.VMEM((n_users, height, width), F32),
            pltpu.VMEM((n_items, half, width), F32),
            pltpu.VMEM((n_users, half, width), BF),
            pltpu.VMEM((n_items - 2 * RING, half, width), BF),
            pltpu.VMEM((128, 128), F32),
            pltpu.SMEM((256,), jnp.int32),
            pltpu.SemaphoreType.DMA((8,)),
            pltpu.SemaphoreType.DMA((4,)),
        ],
        compiler_params=pltpu.CompilerParams(vmem_limit_bytes=56 * 2**20),
        cost_estimate=pl.CostEstimate(flops=13 * 10**9, bytes_accessed=20 * 2**20, transcendentals=2 * 10**7),
    )(place, table, scalars, own_users, near_users, far_users, items_in)


def device(x, y, z, core):
    return (((x % RING) * RING + y % RING) * RING + z % RING) * 2 + core


def every():
    return [(x, y, z, c) for x in range(RING) for y in range(RING) for z in range(RING) for c in range(2)]


AXES = ("x", "y", "z", "n")


def along_z(a, d):
    return lax.ppermute(a, AXES, [(device(x, y, z, c), device(x, y, z + d, c)) for x, y, z, c in every()])


def along_first(a, d):
    return lax.ppermute(a, AXES, [
        (device(x, y, z, c), device(x + (d if c else 0), y + (0 if c else d), z, c)) for x, y, z, c in every()])


def along_second(a, d):
    return lax.ppermute(a, AXES, [
        (device(x, y, z, c), device(x + (0 if c else d), y + (d if c else 0), z, c)) for x, y, z, c in every()])


def across(a):
    return lax.ppermute(a, AXES, [(device(x, y, z, c), device(x, y, z, 1 - c)) for x, y, z, c in every()])


def body(user_emb, item_emb, pairs, counts, natural_exponent_param, additive_shift_param):
    my_x, my_y, my_z = lax.axis_index("x"), lax.axis_index("y"), lax.axis_index("z")
    core = lax.axis_index("n")
    blocks, height, width = user_emb.shape
    half = height // 2
    sharpness = jnp.exp(natural_exponent_param[0])
    shift = additive_shift_param[0]
    root = height ** 0.5

    users_low = user_emb.astype(BF)
    my_half = lax.dynamic_slice_in_dim(user_emb, core * half, half, axis=1).astype(BF)
    slots = pairs.shape[1]
    flat = jnp.concatenate([pairs[0].reshape(-1), counts]).astype(F32)
    flat = jnp.pad(flat, (0, 16 * width - flat.shape[0])).astype(BF).reshape(16, width)
    packet = jnp.concatenate([my_half.reshape(blocks * half, width), flat], axis=0)
    items_low = item_emb.astype(BF)

    got = [along_z(packet, d) for d in (1, 2, 3)]
    line = jnp.concatenate([items_low] + [along_first(items_low, d) for d in (1, 2, 3)], axis=0)
    plane = jnp.concatenate([line] + [along_second(line, d) for d in (1, 2, 3)], axis=0)
    near = jnp.concatenate([g[: blocks * half].reshape(blocks, half, width) for g in got], axis=0)
    far = across(near)
    lists = [g[blocks * half:].reshape(-1)[: slots * 3 + 1].astype(jnp.int32) for g in [packet] + got]
    table = jnp.concatenate([v[: slots * 3] for v in lists] + [v[slots * 3:] for v in lists])
    place = jnp.stack([my_x, my_y, my_z, core]).astype(jnp.int32)
    scalars = jnp.stack([sharpness * LOG2E, shift * LOG2E, sharpness * height ** -0.5, jnp.float32(root)])

    user_keep, user_give, item_keep, item_give, sums = score(
        place, table, scalars, users_low, near, far, plane)

    user_got = across(user_give)
    summed = user_keep + user_got.astype(F32)
    back = [along_z(summed[d * blocks:(d + 1) * blocks].astype(BF), -d) for d in (1, 2, 3)]
    user_half = summed[:blocks] + back[0].astype(F32) + back[1].astype(F32) + back[2].astype(F32)
    user_rest = across(user_half)
    low = jnp.where(core == 0, user_half, user_rest)
    high = jnp.where(core == 0, user_rest, user_half)
    user_grad = jnp.concatenate([low, high], axis=1)

    n = 2 * RING
    back = [along_second(item_give[(d - 1) * n: d * n], -d) for d in (1, 2, 3)]
    item_line = item_keep + back[0].astype(F32) + back[1].astype(F32) + back[2].astype(F32)
    back = [along_first(item_line[2 * d: 2 * d + 2].astype(BF), -d) for d in (1, 2, 3)]
    item_grad = item_line[:2] + back[0].astype(F32) + back[1].astype(F32) + back[2].astype(F32)

    totals = jnp.concatenate([jnp.sum(sums, axis=(1, 2)), counts.astype(F32) * 0.5])
    totals = lax.psum(totals, AXES)
    objective = totals[:3] / (height * height * totals[3])
    return user_grad, item_grad, objective


def solution(mesh):
    grid = Mesh(mesh.devices.reshape(RING, RING, RING, 2), AXES)
    return jax.shard_map(
        body,
        mesh=grid,
        in_specs=(P(WIDE, None, None), P(WIDE, "n", None), P(WIDE, None, None), P(WIDE), P(), P()),
        out_specs=(P(WIDE, None, None), P(WIDE, "n", None), P()),
        check_vma=False,
    )
```

```python
import functools

import jax
import jax.numpy as jnp
from jax import lax
from jax.experimental import pallas as pl
from jax.experimental.pallas import tpu as pltpu
from jax.sharding import Mesh
from jax.sharding import PartitionSpec as P

LOG2E = 1.4426950408889634
RING = 4
NT = (((1,), (1,)), ((), ()))
NN = (((1,), (0,)), ((), ()))
TN = (((0,), (0,)), ((), ()))
WIDE = ("x", "y", "z")
BF = jnp.bfloat16
F32 = jnp.float32


def score_kernel(
    place, scalars, own, ring_a, ring_b, ring_c, over_a, over_b, over_c, line, second_1, second_2, second_3,
    keep_2, keep_late, keep_early, own_out, give_2, give_early, give_late,
    item_keep, item_give_1, item_give_2, item_give_3, sums,
    users, items, uacc, iacc, ugive, igive, eye, jobs, rows_low, rows_int, table, in_sem, out_sem, table_sem,
):
    my_x, my_y, my_z, core = place[0], place[1], place[2], place[3]
    blocks, half, width = keep_2.shape
    mine = pl.multiple_of(core * half, half)
    other = pl.multiple_of((1 - core) * half, half)
    near = jnp.where(core == 0, 1, RING - 1)
    far = RING - near
    body_rows = blocks * half
    lists = []
    for k, (packet, first, d) in enumerate(
            [(own, 2 * body_rows, 0), (ring_a, body_rows, near), (over_a, body_rows, far), (ring_c, body_rows, 2)]):
        to = rows_low.at[pl.ds(pl.multiple_of(d * 16, 16), 16), :]
        lists.append(pltpu.make_async_copy(packet.at[pl.ds(first, 16), :], to, table_sem.at[k]))
    for c in lists:
        c.start()
    copies = []
    n = line.shape[0]
    for k, piece in enumerate([line, second_1, second_2, second_3]):
        copies.append(pltpu.make_async_copy(piece, items.at[pl.ds(k * n, n)], in_sem.at[k]))
    moves = [(own, 0, 0, 0), (own, body_rows, 0, half), (ring_a, 0, near, mine), (ring_b, 0, near, other),
             (over_a, 0, far, other), (over_b, 0, far, mine), (ring_c, 0, 2, mine), (over_c, 0, 2, other)]
    for k, (packet, first, d, at) in enumerate(moves):
        for b in range(blocks):
            copies.append(pltpu.make_async_copy(
                packet.at[pl.ds(first + b * half, half), :],
                users.at[d * blocks + b, pl.ds(at, half), :], in_sem.at[4 + k * blocks + b]))
    for c in copies:
        c.start()

    for c in lists:
        c.wait()
    rows_int[...] = rows_low[...].astype(F32).astype(jnp.int32)
    to_smem = pltpu.make_async_copy(rows_int, table, table_sem.at[4])
    to_smem.start()
    uacc[...] = jnp.zeros_like(uacc)
    iacc[...] = jnp.zeros_like(iacc)
    row = lax.broadcasted_iota(jnp.int32, (128, 128), 0)
    col = lax.broadcasted_iota(jnp.int32, (128, 128), 1)
    eye[...] = (row == col).astype(F32)
    to_smem.wait()
    count = jnp.int32(0)
    for d in range(RING):
        live_slots = table[16 * d + 3, 0]

        def list_slot(slot, count, d=d, live_slots=live_slots):
            user, item, label = table[16 * d, slot], table[16 * d + 1, slot], table[16 * d + 2, slot]
            dx = (my_x - (item >> 5)) & 3
            dy = (my_y - (item >> 3)) & 3
            first = jnp.where(core == 0, dy, dx)
            second = jnp.where(core == 0, dx, dy)
            jobs[count] = d * blocks + (user & (blocks - 1))
            jobs[count + 72] = (second * RING + first) * 2 + (item & 1)
            jobs[count + 144] = label
            live = (((item >> 1) & 3) == my_z) & (slot < live_slots)
            return count + live.astype(jnp.int32)

        count = lax.fori_loop(0, 64, list_slot, count, unroll=4)
    jobs[count] = 0
    jobs[count + 72] = 0
    jobs[count + 144] = 0
    for c in copies:
        c.wait()

    slope, shift, gain = scalars[0], scalars[1], scalars[2]

    def tile(u, it, slope_j, shift_j, label_j):
        inner = lax.dot_general(u, it, NT, preferred_element_type=F32)
        x = inner * slope_j + shift_j
        e = jnp.exp2(-jnp.abs(x))
        t = 1.0 + e
        high = x >= 0.0
        num = jnp.where(high, 1.0, e)
        soft = jnp.maximum(x, 0.0)
        if label_j is not None:
            hit = eye[...] * label_j > 0.5
            nums, softs = [], []
            for q in range(2):
                r = slice(q * 128, (q + 1) * 128)
                xb, eb = x[r, r], e[r, r]
                nb = jnp.where(hit, jnp.where(high[r, r], -eb, -1.0), num[r, r])
                sb = soft[r, r] - jnp.where(hit, xb, 0.0)
                keep = slice((1 - q) * 128, (2 - q) * 128)
                nums.append(jnp.concatenate([nb, num[r, keep]] if q == 0 else [num[r, keep], nb], axis=1))
                softs.append(jnp.concatenate([sb, soft[r, keep]] if q == 0 else [soft[r, keep], sb], axis=1))
            num = jnp.concatenate(nums, axis=0)
            soft = jnp.concatenate(softs, axis=0)
        w = num * pl.reciprocal(t, approx=True)
        scaled = (w * gain).astype(BF)
        tt = t.reshape(8, 32, 256)
        ee = e.reshape(8, 32, 256)
        prod = ee[0]
        for m in range(1, 8):
            prod = prod * tt[m] + ee[m]
        pr = prod.reshape(4, 8, 256)
        p0 = pr[0] + pr[1] + pr[0] * pr[1]
        p1 = pr[2] + pr[3] + pr[2] * pr[3]
        p = p0 + p1 + p0 * p1
        logs = jnp.where(p < 1e-3, p * (1.0 - 0.5 * p), jnp.log(1.0 + p))
        soft_sum = soft.reshape(32, 8, 256).sum(0)
        w_sum = w.reshape(32, 8, 256).sum(0)
        return scaled, soft_sum, logs, w_sum

    def one_job(j, valid, carry):
        soft_acc, log_acc, w_acc = carry
        ui, ii = jobs[j], jobs[j + 72]
        label_j = jobs[j + 144].astype(F32)
        slope_j = jnp.where(valid, slope, 0.0)
        shift_j = jnp.where(valid, shift, -1e30)
        label_j = jnp.where(valid, label_j, 0.0)
        it = items[ii]
        um = users[ui, pl.ds(mine, half), :]
        uo = users[ui, pl.ds(other, half), :]
        sm, a0, l0, w0 = tile(um, it, slope_j, shift_j, label_j)
        so, a1, l1, w1 = tile(uo, it, slope_j, shift_j, None)
        uacc[ui, pl.ds(mine, half), :] += lax.dot_general(sm, it, NN, preferred_element_type=F32)
        uacc[ui, pl.ds(other, half), :] += lax.dot_general(so, it, NN, preferred_element_type=F32)
        iacc[ii] += (lax.dot_general(sm, um, TN, preferred_element_type=F32)
                     + lax.dot_general(so, uo, TN, preferred_element_type=F32))
        return soft_acc + (a0 + a1), log_acc + (l0 + l1), w_acc + (w0 + w1)

    def two_jobs(g, carry):
        carry = one_job(2 * g, True, carry)
        return one_job(2 * g + 1, 2 * g + 1 < count, carry)

    zero = jnp.zeros((8, 256), F32)
    soft_acc, log_acc, w_acc = lax.fori_loop(0, (count + 1) // 2, two_jobs, (zero, zero, zero))

    serve = far
    give = near
    out = []

    def send(src, dst):
        c = pltpu.make_async_copy(src, dst, out_sem.at[len(out)])
        c.start()
        out.append(c)

    def rows_of(d, at):
        return uacc.at[pl.ds(d * blocks, blocks), pl.ds(at, half), :]

    def lower(d, at, slot):
        def one(b, none):
            ugive[slot * blocks + b] = uacc[d * blocks + b, pl.ds(at, half), :].astype(BF)
            return none
        lax.fori_loop(0, blocks, one, 0)

    lower(2, other, 0)
    send(ugive.at[pl.ds(0, blocks)], give_2)
    lower(give, mine, 1)
    send(ugive.at[pl.ds(blocks, blocks)], give_early)
    lower(give, other, 2)
    send(ugive.at[pl.ds(2 * blocks, blocks)], give_late)
    send(rows_of(2, mine), keep_2)
    send(rows_of(serve, other), keep_early)
    send(rows_of(serve, mine), keep_late)
    send(uacc.at[pl.ds(0, blocks)], own_out)
    for k, dst in enumerate([item_give_1, item_give_2, item_give_3]):
        def item_out(b, none, k=k):
            igive[k * n + b] = iacc[(k + 1) * n + b].astype(BF)
            return none
        lax.fori_loop(0, n, item_out, 0)
        send(igive.at[pl.ds(k * n, n)], dst)
    send(iacc.at[pl.ds(0, n)], item_keep)

    def scale_sum(b, acc):
        prod = uacc[b] * users[b].astype(F32)
        return acc + prod.reshape(64, 8, 256).sum(0)

    scale_acc = lax.fori_loop(0, RING * blocks, scale_sum, zero)
    total = [soft_acc * (1.0 / LOG2E) + log_acc, scale_acc * scalars[3], w_acc]
    lane = lax.broadcasted_iota(jnp.int32, (8, 128), 1)
    packed = jnp.zeros((8, 128), F32)
    for k in range(3):
        packed = jnp.where(lane == k, jnp.sum(total[k]), packed)
    packed = jnp.where(lane == 3, 0.5 * table[3, 0].astype(F32), packed)
    sums[...] = packed
    for c in out:
        c.wait()


def score(place, scalars, pieces):
    n, half, width = pieces[7].shape
    blocks = 4
    height = 2 * half
    n_users, n_items = RING * blocks, RING * n
    smem = pl.BlockSpec(memory_space=pltpu.SMEM)
    any_ = pl.BlockSpec(memory_space=pl.ANY)
    part = (blocks, half, width)
    return pl.pallas_call(
        score_kernel,
        in_specs=[smem, smem] + [any_] * 11,
        out_specs=[any_] * 11 + [pl.BlockSpec(memory_space=pltpu.VMEM)],
        out_shape=[jax.ShapeDtypeStruct(part, F32)] * 3 + [jax.ShapeDtypeStruct((blocks, height, width), F32)]
        + [jax.ShapeDtypeStruct(part, BF)] * 3
        + [jax.ShapeDtypeStruct((n, half, width), F32)] + [jax.ShapeDtypeStruct((n, half, width), BF)] * 3
        + [jax.ShapeDtypeStruct((8, 128), F32)],
        scratch_shapes=[
            pltpu.VMEM((n_users, height, width), BF),
            pltpu.VMEM((n_items, half, width), BF),
            pltpu.VMEM((n_users, height, width), F32),
            pltpu.VMEM((n_items, half, width), F32),
            pltpu.VMEM((3 * blocks, half, width), BF),
            pltpu.VMEM((n_items - n, half, width), BF),
            pltpu.VMEM((128, 128), F32),
            pltpu.SMEM((256,), jnp.int32),
            pltpu.VMEM((64, width), BF),
            pltpu.VMEM((64, width), jnp.int32),
            pltpu.SMEM((64, width), jnp.int32),
            pltpu.SemaphoreType.DMA((40,)),
            pltpu.SemaphoreType.DMA((16,)),
            pltpu.SemaphoreType.DMA((5,)),
        ],
        compiler_params=pltpu.CompilerParams(vmem_limit_bytes=56 * 2**20),
        cost_estimate=pl.CostEstimate(flops=13 * 10**9, bytes_accessed=20 * 2**20, transcendentals=2 * 10**7),
    )(place, scalars, *pieces)


def device(x, y, z, core):
    return (((x % RING) * RING + y % RING) * RING + z % RING) * 2 + core


def every():
    return [(x, y, z, c) for x in range(RING) for y in range(RING) for z in range(RING) for c in range(2)]


AXES = ("x", "y", "z", "n")


def along_z(a):
    return lax.ppermute(a, AXES, [
        (device(x, y, z, c), device(x, y, z + (-1 if c else 1), c)) for x, y, z, c in every()])


def swap(a, bit):
    return lax.ppermute(a, AXES, [(i, i ^ bit) for i in range(128)])


def along_first(a, d):
    return lax.ppermute(a, AXES, [
        (device(x, y, z, c), device(x + (d if c else 0), y + (0 if c else d), z, c)) for x, y, z, c in every()])


def along_second(a, d):
    return lax.ppermute(a, AXES, [
        (device(x, y, z, c), device(x + (0 if c else d), y + (d if c else 0), z, c)) for x, y, z, c in every()])


def across(a):
    return lax.ppermute(a, AXES, [(device(x, y, z, c), device(x, y, z, 1 - c)) for x, y, z, c in every()])


def body(user_emb, item_emb, pairs, counts, natural_exponent_param, additive_shift_param):
    my_x, my_y, my_z = lax.axis_index("x"), lax.axis_index("y"), lax.axis_index("z")
    core = lax.axis_index("n")
    blocks, height, width = user_emb.shape
    half = height // 2
    sharpness = jnp.exp(natural_exponent_param[0])
    shift = additive_shift_param[0]
    place = jnp.stack([my_x, my_y, my_z, core]).astype(jnp.int32)
    scalars = jnp.stack([sharpness * LOG2E, shift * LOG2E, sharpness * height ** -0.5, jnp.float32(height ** 0.5)])

    slots = pairs.shape[1]
    rows = jnp.concatenate([pairs[0].T, jnp.broadcast_to(counts[:, None], (1, slots))], axis=0)
    rows = jnp.pad(rows.astype(F32), ((0, 12), (0, width - slots))).astype(BF)
    lower = [user_emb[:, :half].astype(BF).reshape(blocks * half, width),
             user_emb[:, half:].astype(BF).reshape(blocks * half, width)]
    own = jnp.concatenate(lower + [rows], axis=0)
    items_low = item_emb.astype(BF)
    halves = user_emb.reshape(blocks, 2, half, width)
    mine = lax.dynamic_index_in_dim(halves, core, 1, keepdims=False).astype(BF).reshape(blocks * half, width)
    other = lax.dynamic_index_in_dim(halves, 1 - core, 1, keepdims=False).astype(BF).reshape(blocks * half, width)

    ring_a = along_z(jnp.concatenate([mine, rows], axis=0))
    ring_b = along_z(other)
    ring_c = along_z(ring_a)
    over_a, over_b, over_c = across(ring_a), across(ring_b), across(ring_c)
    line = jnp.concatenate([items_low] + [along_first(items_low, d) for d in (1, 2, 3)], axis=0)
    second = [along_second(line, d) for d in (1, 2, 3)]

    (keep_2, keep_late, keep_early, own_part, give_2, give_early, give_late,
     item_keep, item_give_1, item_give_2, item_give_3, sums) = score(
        place, scalars, [own, ring_a, ring_b, ring_c, over_a, over_b, over_c, line] + second)

    for bit in (1, 2, 4, 8, 16, 32, 64):
        sums = sums + swap(sums, bit)
    totals = sums[0]
    objective = totals[:3] / (height * height * totals[3])

    back = [along_second(g, -d) for d, g in ((1, item_give_1), (2, item_give_2), (3, item_give_3))]
    item_line = item_keep + back[0].astype(F32) + back[1].astype(F32) + back[2].astype(F32)
    back = [along_first(item_line[2 * d: 2 * d + 2].astype(BF), -d) for d in (1, 2, 3)]
    item_grad = item_line[:2] + back[0].astype(F32) + back[1].astype(F32) + back[2].astype(F32)

    relay = along_z((keep_2 + across(give_2).astype(F32)).astype(BF))
    early = along_z((keep_early + across(give_early).astype(F32)).astype(BF))
    late = along_z((keep_late + across(give_late).astype(F32) + relay.astype(F32)).astype(BF))
    own_sum = own_part + across(own_part)
    early_over, late_over = across(early), across(late)
    first_core = core == 0
    low_a, low_b = jnp.where(first_core, late, late_over), jnp.where(first_core, early_over, early)
    high_a, high_b = jnp.where(first_core, early, early_over), jnp.where(first_core, late_over, late)
    user_grad = own_sum + jnp.concatenate(
        [low_a.astype(F32) + low_b.astype(F32), high_a.astype(F32) + high_b.astype(F32)], axis=1)
    return user_grad, item_grad, objective


def solution(mesh):
    grid = Mesh(mesh.devices.reshape(RING, RING, RING, 2), AXES)
    return jax.shard_map(
        body,
        mesh=grid,
        in_specs=(P(WIDE, None, None), P(WIDE, "n", None), P(WIDE, None, None), P(WIDE), P(), P()),
        out_specs=(P(WIDE, None, None), P(WIDE, "n", None), P()),
        check_vma=False,
    )
```

```python
import functools

import jax
import jax.numpy as jnp
from jax import lax
from jax.experimental import pallas as pl
from jax.experimental.pallas import tpu as pltpu
from jax.sharding import Mesh
from jax.sharding import PartitionSpec as P

LOG2E = 1.4426950408889634
RING = 4
NT = (((1,), (1,)), ((), ()))
NN = (((1,), (0,)), ((), ()))
TN = (((0,), (0,)), ((), ()))
WIDE = ("x", "y", "z")
BF = jnp.bfloat16
F32 = jnp.float32


def plan_kernel(place, own, ring, ring_2, over, *rest):
    jobs, rows_low, sem = rest[-3:]
    my_x, my_y, my_z, core = place[0], place[1], place[2], place[3]
    near = jnp.where(core == 0, 1, RING - 1)
    copies = []
    for k, (packet, d) in enumerate([(own, 0), (ring, near), (over, RING - near), (ring_2, 2)]):
        to = rows_low.at[pl.ds(pl.multiple_of(d * 16, 16), 16), :]
        copies.append(pltpu.make_async_copy(packet.at[pl.ds(packet.shape[0] - 16, 16), :], to, sem.at[k]))
    for c in copies:
        c.start()
    for c in copies:
        c.wait()
    width = rows_low.shape[1]
    owner_id = lax.broadcasted_iota(jnp.int32, (16, width), 0)
    slot = lax.broadcasted_iota(jnp.int32, (16, width), 1)
    lane = lax.broadcasted_iota(jnp.int32, (16, 128), 1)
    for d in range(RING):
        rows = rows_low[16 * d: 16 * d + 16, :].astype(F32)
        user, item, label = (jnp.broadcast_to(rows[k: k + 1], (16, width)) for k in range(3))
        live_slots = jnp.broadcast_to(rows[3:4, :1], (16, width))
        item = item.astype(jnp.int32)
        mine = (((item >> 1) & 3) == my_z) & ((item >> 3) == owner_id) & (slot.astype(F32) < live_slots)
        dx = (my_x - (item >> 5)) & 3
        dy = (my_y - ((item >> 3) & 3)) & 3
        at = jnp.where(core == 0, dx * 4 + dy, dy * 4 + dx) * 2 + (item & 1)
        block = d * 4 + (user.astype(jnp.int32) & 3)
        out = jnp.zeros((16, 128), F32)
        for k, v in enumerate([block.astype(F32), at.astype(F32), label, jnp.ones_like(label)]):
            out = jnp.where(lane == k, jnp.sum(jnp.where(mine, v, 0.0), axis=1, keepdims=True), out)
        if d == 0:
            out = jnp.where(lane == 4, live_slots[:, :128], out)
        jobs[16 * d: 16 * d + 16, :] = out.astype(jnp.int32)


def plan(place, own, ring, ring_2, over, *before):
    hbm = pl.BlockSpec(memory_space=pl.ANY)
    width = own.shape[1]
    return pl.pallas_call(
        plan_kernel,
        in_specs=[pl.BlockSpec(memory_space=pltpu.SMEM)] + [hbm] * (4 + len(before)),
        out_specs=pl.BlockSpec(memory_space=pltpu.VMEM),
        out_shape=jax.ShapeDtypeStruct((64, 128), jnp.int32),
        scratch_shapes=[pltpu.VMEM((64, width), BF), pltpu.SemaphoreType.DMA((4,))],
        compiler_params=pltpu.CompilerParams(vmem_limit_bytes=2**20),
        cost_estimate=pl.CostEstimate(flops=10**6, bytes_accessed=2**20, transcendentals=0),
    )(place, own, ring, ring_2, over, *before)


def score_kernel(
    place, jobs, scalars, own, ring, ring_2, over, line_a, line_b, up_a, up_b, down_a, down_b, up_2, down_2,
    keep_2, keep_late, keep_early, give,
    item_keep, item_up, item_down, item_up_low, item_down_low, item_relay_up, item_relay_down, sums,
    users, items, uacc, iacc, ugive, igive, eye, in_sem, out_sem,
):
    core = place[3]
    blocks, half, width = keep_2.shape
    mine = pl.multiple_of(core * half, half)
    other = pl.multiple_of((1 - core) * half, half)
    near = jnp.where(core == 0, 1, RING - 1)
    far = RING - near
    body_rows = blocks * half
    copies = []
    h = line_a.shape[0]
    n = 2 * h
    for k, (piece, at) in enumerate([
            (line_a, 0), (line_b, h), (up_a, n), (up_b, n + h), (down_b, 3 * n), (down_a, 3 * n + h),
            (up_2, 2 * n), (down_2, 2 * n + h)]):
        copies.append(pltpu.make_async_copy(piece, items.at[pl.ds(at, piece.shape[0])], in_sem.at[k]))
    moves = [(own, 0, 0, 0), (own, body_rows, 0, half), (ring, 0, near, 0), (ring, body_rows, near, half),
             (over, body_rows + 16, far, 0), (over, 2 * body_rows + 16, far, half), (ring_2, 0, 2, mine),
             (over, 0, 2, other)]
    for k, (packet, first, d, at) in enumerate(moves):
        for b in range(blocks):
            copies.append(pltpu.make_async_copy(
                packet.at[pl.ds(first + b * half, half), :],
                users.at[d * blocks + b, pl.ds(at, half), :], in_sem.at[8 + k * blocks + b]))
    for c in copies:
        c.start()

    uacc[...] = jnp.zeros_like(uacc)
    iacc[...] = jnp.zeros_like(iacc)
    row = lax.broadcasted_iota(jnp.int32, (128, 128), 0)
    col = lax.broadcasted_iota(jnp.int32, (128, 128), 1)
    eye[...] = (row == col).astype(F32)
    for c in copies:
        c.wait()

    slope, shift, gain = scalars[0], scalars[1], scalars[2]

    def tile(u, it, slope_j, shift_j, label_j):
        inner = lax.dot_general(u, it, NT, preferred_element_type=F32)
        y = inner * slope_j + shift_j
        w = pl.reciprocal(1.0 + jnp.exp2(y), approx=True)
        less = 1.0 - w
        near_one = jnp.maximum(w, less)
        low = jnp.minimum(y, 0.0)
        if label_j is not None:
            hit = eye[...] * label_j > 0.5
            ws, lows = [], []
            for q in range(2):
                r = slice(q * 128, (q + 1) * 128)
                keep = slice((1 - q) * 128, (2 - q) * 128)
                wb = jnp.where(hit, -less[r, r], w[r, r])
                lb = jnp.minimum(jnp.where(hit, -y[r, r], y[r, r]), 0.0)
                ws.append(jnp.concatenate([wb, w[r, keep]] if q == 0 else [w[r, keep], wb], axis=1))
                lows.append(jnp.concatenate([lb, low[r, keep]] if q == 0 else [low[r, keep], lb], axis=1))
            w = jnp.concatenate(ws, axis=0)
            low = jnp.concatenate(lows, axis=0)
        scaled = (w * gain).astype(BF)
        nn = near_one.reshape(32, 8, 256)
        logs = jnp.log2(functools.reduce(lambda p, m: p * nn[m], range(1, 32), nn[0]))
        soft_sum = low.reshape(32, 8, 256).sum(0)
        w_sum = w.reshape(32, 8, 256).sum(0)
        return scaled, soft_sum, logs, w_sum

    def one_job(j, carry):
        soft_acc, log_acc, w_acc = carry
        ui, ii, live = jobs[j, 0], jobs[j, 1], jobs[j, 3] == 1
        label_j = jobs[j, 2].astype(F32)
        slope_j = jnp.where(live, slope, 0.0)
        shift_j = jnp.where(live, shift, 1e30)
        it = items[ii]
        um = users[ui, pl.ds(mine, half), :]
        uo = users[ui, pl.ds(other, half), :]
        sm, a0, l0, w0 = tile(um, it, slope_j, shift_j, label_j)
        so, a1, l1, w1 = tile(uo, it, slope_j, shift_j, None)
        uacc[ui, pl.ds(mine, half), :] += lax.dot_general(sm, it, NN, preferred_element_type=F32)
        uacc[ui, pl.ds(other, half), :] += lax.dot_general(so, it, NN, preferred_element_type=F32)
        iacc[ii] += (lax.dot_general(sm, um, TN, preferred_element_type=F32)
                     + lax.dot_general(so, uo, TN, preferred_element_type=F32))
        return soft_acc + (a0 + a1), log_acc + (l0 + l1), w_acc + (w0 + w1)

    turn = 4

    def some_jobs(g, carry):
        for k in range(turn):
            carry = one_job(turn * g + k, carry)
        return carry

    zero = jnp.zeros((8, 256), F32)
    soft_acc, log_acc, w_acc = lax.fori_loop(0, jobs.shape[0] // turn, some_jobs, (zero, zero, zero))

    out = []

    def send(src, dst):
        c = pltpu.make_async_copy(src, dst, out_sem.at[len(out)])
        c.start()
        out.append(c)

    def rows_of(d, at):
        return uacc.at[pl.ds(d * blocks, blocks), pl.ds(at, half), :]

    def lower(d, at, slot):
        def one(b, none):
            ugive[slot * blocks + b] = uacc[d * blocks + b, pl.ds(at, half), :].astype(BF)
            return none
        lax.fori_loop(0, blocks, one, 0)

    def item_lower(first, count, at, dst):
        def one(b, none):
            igive[at + b] = iacc[first + b].astype(BF)
            return none
        lax.fori_loop(0, count, one, 0)
        send(igive.at[pl.ds(at, count)], dst)

    item_lower(2 * n, h, 0, item_relay_down)
    item_lower(2 * n + h, h, h, item_relay_up)
    lower(2, other, 0)
    lower(near, mine, 1)
    lower(near, other, 2)

    def own_lower(b, none):
        for k in range(2):
            ugive[3 * blocks + 2 * b + k] = uacc[b, k * half: (k + 1) * half, :].astype(BF)
        return none

    lax.fori_loop(0, blocks, own_lower, 0)
    send(ugive, give)
    send(iacc.at[pl.ds(n, h)], item_down)
    send(iacc.at[pl.ds(3 * n + h, h)], item_up)
    item_lower(n + h, h, 2 * h, item_down_low)
    item_lower(3 * n, h, 3 * h, item_up_low)
    send(iacc.at[pl.ds(0, n)], item_keep)
    send(rows_of(2, mine), keep_2)
    send(rows_of(far, other), keep_early)
    send(rows_of(far, mine), keep_late)

    def scale_sum(b, acc):
        prod = uacc[b] * users[b].astype(F32)
        return acc + prod.reshape(64, 8, 256).sum(0)

    scale_acc = lax.fori_loop(0, RING * blocks, scale_sum, zero)
    total = [(soft_acc + log_acc) * (-1.0 / LOG2E), scale_acc * scalars[3], w_acc]
    lane = lax.broadcasted_iota(jnp.int32, (8, 256), 1)
    packed = jnp.zeros((8, 256), F32)
    for k in range(3):
        packed = jnp.where(lane == k, jnp.sum(total[k]), packed)
    packed = jnp.where(lane == 3, 0.5 * jobs[0, 4].astype(F32), packed)
    sums[...] = packed
    for c in out:
        c.wait()


def score(place, jobs, scalars, pieces):
    n, half, width = pieces[4].shape
    n = 2 * n
    blocks = 4
    height = 2 * half
    n_users, n_items = RING * blocks, RING * n
    smem = pl.BlockSpec(memory_space=pltpu.SMEM)
    any_ = pl.BlockSpec(memory_space=pl.ANY)
    part = (blocks, half, width)
    return pl.pallas_call(
        score_kernel,
        in_specs=[smem, smem, smem] + [any_] * len(pieces),
        out_specs=[any_] * 11 + [pl.BlockSpec(memory_space=pltpu.VMEM)],
        out_shape=[jax.ShapeDtypeStruct(part, F32)] * 3 + [jax.ShapeDtypeStruct((5 * blocks, half, width), BF)]
        + [jax.ShapeDtypeStruct((n, half, width), F32)] + [jax.ShapeDtypeStruct((n // 2, half, width), F32)] * 2
        + [jax.ShapeDtypeStruct((n // 2, half, width), BF)] * 4
        + [jax.ShapeDtypeStruct((8, width), F32)],
        scratch_shapes=[
            pltpu.VMEM((n_users, height, width), BF),
            pltpu.VMEM((n_items, half, width), BF),
            pltpu.VMEM((n_users, height, width), F32),
            pltpu.VMEM((n_items, half, width), F32),
            pltpu.VMEM((5 * blocks, half, width), BF),
            pltpu.VMEM((2 * n, half, width), BF),
            pltpu.VMEM((128, 128), F32),
            pltpu.SemaphoreType.DMA((48,)),
            pltpu.SemaphoreType.DMA((16,)),
        ],
        compiler_params=pltpu.CompilerParams(vmem_limit_bytes=36 * 2**20),
        cost_estimate=pl.CostEstimate(flops=13 * 10**9, bytes_accessed=20 * 2**20, transcendentals=2 * 10**7),
    )(place, jobs, scalars, *pieces)


def finish_kernel(place, give, given, early, late, early_over, late_over, out):
    first = place[3] == 0
    half = early.shape[1]
    for k, (ours, theirs) in enumerate([((late, early_over), (late_over, early)), ((early, late_over), (early_over, late))]):
        a = jnp.where(first, ours[0][0].astype(F32), theirs[0][0].astype(F32))
        b = jnp.where(first, ours[1][0].astype(F32), theirs[1][0].astype(F32))
        own = give[k].astype(F32) + given[k].astype(F32)
        out[0, k * half: (k + 1) * half, :] = own + (a + b)


def finish(place, give, given, early, late, early_over, late_over):
    blocks, half, width = early.shape
    own = pl.BlockSpec((2, half, width), lambda b: (3 * blocks // 2 + b, 0, 0))
    part = pl.BlockSpec((1, half, width), lambda b: (b, 0, 0))
    return pl.pallas_call(
        finish_kernel,
        grid=(blocks,),
        in_specs=[pl.BlockSpec(memory_space=pltpu.SMEM), own, own, part, part, part, part],
        out_specs=pl.BlockSpec((1, 2 * half, width), lambda b: (b, 0, 0)),
        out_shape=jax.ShapeDtypeStruct((blocks, 2 * half, width), F32),
        compiler_params=pltpu.CompilerParams(vmem_limit_bytes=8 * 2**20),
        cost_estimate=pl.CostEstimate(flops=2 * 10**6, bytes_accessed=6 * 2**20, transcendentals=0),
    )(place, give, given, early, late, early_over, late_over)


def device(x, y, z, core):
    return (((x % RING) * RING + y % RING) * RING + z % RING) * 2 + core


def every():
    return [(x, y, z, c) for x in range(RING) for y in range(RING) for z in range(RING) for c in range(2)]


AXES = ("x", "y", "z", "n")


def named(f):
    def call(a, *rest, name):
        with jax.named_scope(name):
            return f(a, *rest)
    return call


@named
def along_z(a):
    return lax.ppermute(a, AXES, [
        (device(x, y, z, c), device(x, y, z + (-1 if c else 1), c)) for x, y, z, c in every()])


@named
def swap(a, bit):
    return lax.ppermute(a, AXES, [(i, i ^ bit) for i in range(128)])


@named
def along_first(a, d):
    return lax.ppermute(a, AXES, [
        (device(x, y, z, c), device(x + (d if c else 0), y + (0 if c else d), z, c)) for x, y, z, c in every()])


@named
def along_second(a, d):
    return lax.ppermute(a, AXES, [
        (device(x, y, z, c), device(x + (0 if c else d), y + (d if c else 0), z, c)) for x, y, z, c in every()])


@named
def across(a):
    return lax.ppermute(a, AXES, [(device(x, y, z, c), device(x, y, z, 1 - c)) for x, y, z, c in every()])


def body(user_emb, item_emb, pairs, counts, natural_exponent_param, additive_shift_param):
    my_x, my_y, my_z = lax.axis_index("x"), lax.axis_index("y"), lax.axis_index("z")
    core = lax.axis_index("n")
    blocks, height, width = user_emb.shape
    half = height // 2
    sharpness = jnp.exp(natural_exponent_param[0])
    shift = additive_shift_param[0]
    place = jnp.stack([my_x, my_y, my_z, core]).astype(jnp.int32)
    scalars = jnp.stack([-sharpness * LOG2E, -shift * LOG2E, sharpness * height ** -0.5, jnp.float32(height ** 0.5)])

    slots = pairs.shape[1]
    rows = jnp.concatenate([pairs[0].T, jnp.broadcast_to(counts[:, None], (1, slots))], axis=0)
    rows = jnp.pad(rows.astype(F32), ((0, 12), (0, width - slots))).astype(BF)
    lower = [user_emb[:, :half].astype(BF).reshape(blocks * half, width),
             user_emb[:, half:].astype(BF).reshape(blocks * half, width)]
    own = jnp.concatenate(lower + [rows], axis=0)
    items_low = item_emb.astype(BF)

    line = [items_low] + [along_first(items_low, d, name="items_line") for d in (1, 2, 3)]
    line_a, line_b = jnp.concatenate(line[:2], axis=0), jnp.concatenate(line[2:], axis=0)
    h = line_a.shape[0]
    up_a, down_a = along_second(line_a, 1, name="items_up_a"), along_second(line_b, -1, name="items_down_a")
    up_b, down_b = along_second(line_b, 1, name="items_up_b"), along_second(line_a, -1, name="items_down_b")
    up_2, down_2 = along_second(up_a, 1, name="items_up_2"), along_second(down_a, -1, name="items_down_2")
    ring = along_z(own, name="users_ring")
    n_rows = blocks * half
    mine = lax.dynamic_slice_in_dim(ring, core * n_rows, n_rows, axis=0)
    ring_2 = along_z(jnp.concatenate([mine, ring[2 * n_rows:]], axis=0), name="users_ring_2")
    lists = ring_2[n_rows:] + (up_a[0, :16] + down_a[0, :16] + up_b[0, :16] + down_b[0, :16]) * 0
    over = across(jnp.concatenate([ring_2[:n_rows], lists, ring], axis=0), name="users_over")

    jobs = plan(place, own, ring, ring_2, over, up_b, down_b)
    (keep_2, keep_late, keep_early, give,
     item_keep, item_up, item_down, item_up_low, item_down_low, item_relay_up, item_relay_down, sums) = score(
        place, jobs, scalars, [own, ring, ring_2, over, line_a, line_b, up_a, up_b, down_a, down_b, up_2, down_2])

    given = across(give, name="give")

    steps = []
    for k in range(7):
        if k == 3:
            sums = sums + given[0, :8].astype(F32) * 0.0
        sums = sums + swap(sums, 1 << k, name="totals_" + str(k))
        steps.append(sums)
    objective = sums[0, :3] / (height * height * sums[0, 3])

    def after(step, a):
        return (a.reshape(-1, 8, width) + steps[step - 1] * 0.0).reshape(a.shape)

    from_up = along_second(item_relay_down, -1, name="item_relay_down")
    from_down = along_second(item_relay_up, 1, name="item_relay_up")
    item_down = jnp.concatenate([after(3, item_down + from_up.astype(F32)).astype(BF), item_down_low])
    item_up = jnp.concatenate([item_up_low, after(3, item_up + from_down.astype(F32)).astype(BF)])
    item_down = along_second(item_down, -1, name="item_down")
    item_up = along_second(item_up, 1, name="item_up")
    item_line = after(5, item_keep + item_down.astype(F32) + item_up.astype(F32))
    back = [along_first(item_line[2 * d: 2 * d + 2].astype(BF), -d, name="item_back") for d in (1, 2, 3)]
    item_grad = item_line[:2] + back[0].astype(F32) + back[1].astype(F32) + back[2].astype(F32)

    relay = along_z((keep_2 + given[:blocks].astype(F32)).astype(BF), name="user_relay")
    early = along_z((keep_early + given[blocks:2 * blocks].astype(F32)).astype(BF), name="user_early")
    late = along_z((keep_late + early[0, :1].astype(F32) * 0.0 + given[2 * blocks:3 * blocks].astype(F32) + relay.astype(F32)).astype(BF), name="user_late")
    early_over, late_over = across(early, name="early_over"), across(late, name="late_over")
    user_grad = finish(place, give, given, early, late, early_over, late_over)
    return user_grad, item_grad, objective


def solution(mesh):
    grid = Mesh(mesh.devices.reshape(RING, RING, RING, 2), AXES)
    return jax.shard_map(
        body,
        mesh=grid,
        in_specs=(P(WIDE, None, None), P(WIDE, "n", None), P(WIDE, None, None), P(WIDE), P(), P()),
        out_specs=(P(WIDE, None, None), P(WIDE, "n", None), P()),
        check_vma=False,
    )
```

```python
import functools

import jax
import jax.numpy as jnp
from jax import lax
from jax.experimental import pallas as pl
from jax.experimental.pallas import tpu as pltpu
from jax.sharding import Mesh
from jax.sharding import PartitionSpec as P

LOG2E = 1.4426950408889634
RING = 4
NT = (((1,), (1,)), ((), ()))
NN = (((1,), (0,)), ((), ()))
TN = (((0,), (0,)), ((), ()))
WIDE = ("x", "y", "z")
BF = jnp.bfloat16
F32 = jnp.float32


def plan_kernel(place, own, ring, ring_2, over, *rest):
    jobs, rows_low, sem = rest[-3:]
    my_x, my_y, my_z, core = place[0], place[1], place[2], place[3]
    near = jnp.where(core == 0, 1, RING - 1)
    copies = []
    for k, (packet, d) in enumerate([(own, 0), (ring, near), (over, RING - near), (ring_2, 2)]):
        to = rows_low.at[pl.ds(pl.multiple_of(d * 16, 16), 16), :]
        copies.append(pltpu.make_async_copy(packet.at[pl.ds(packet.shape[0] - 16, 16), :], to, sem.at[k]))
    for c in copies:
        c.start()
    for c in copies:
        c.wait()
    width = rows_low.shape[1]
    owner_id = lax.broadcasted_iota(jnp.int32, (16, width), 0)
    slot = lax.broadcasted_iota(jnp.int32, (16, width), 1)
    lane = lax.broadcasted_iota(jnp.int32, (16, 128), 1)
    for d in range(RING):
        rows = rows_low[16 * d: 16 * d + 16, :].astype(F32)
        user, item, label = (jnp.broadcast_to(rows[k: k + 1], (16, width)) for k in range(3))
        live_slots = jnp.broadcast_to(rows[3:4, :1], (16, width))
        item = item.astype(jnp.int32)
        mine = (((item >> 1) & 3) == my_z) & ((item >> 3) == owner_id) & (slot.astype(F32) < live_slots)
        dx = (my_x - (item >> 5)) & 3
        dy = (my_y - ((item >> 3) & 3)) & 3
        at = jnp.where(core == 0, dx * 4 + dy, dy * 4 + dx) * 2 + (item & 1)
        block = d * 4 + (user.astype(jnp.int32) & 3)
        out = jnp.zeros((16, 128), F32)
        for k, v in enumerate([block.astype(F32), at.astype(F32), label, jnp.ones_like(label)]):
            out = jnp.where(lane == k, jnp.sum(jnp.where(mine, v, 0.0), axis=1, keepdims=True), out)
        if d == 0:
            out = jnp.where(lane == 4, live_slots[:, :128], out)
        jobs[16 * d: 16 * d + 16, :] = out.astype(jnp.int32)


def plan(place, own, ring, ring_2, over, *before):
    hbm = pl.BlockSpec(memory_space=pl.ANY)
    width = own.shape[1]
    return pl.pallas_call(
        plan_kernel,
        in_specs=[pl.BlockSpec(memory_space=pltpu.SMEM)] + [hbm] * (4 + len(before)),
        out_specs=pl.BlockSpec(memory_space=pltpu.VMEM),
        out_shape=jax.ShapeDtypeStruct((64, 128), jnp.int32),
        scratch_shapes=[pltpu.VMEM((64, width), BF), pltpu.SemaphoreType.DMA((4,))],
        compiler_params=pltpu.CompilerParams(vmem_limit_bytes=2**20),
        cost_estimate=pl.CostEstimate(flops=10**6, bytes_accessed=2**20, transcendentals=0),
    )(place, own, ring, ring_2, over, *before)


def score_kernel(
    place, jobs, scalars, own, ring, ring_2, over, line_a, line_b, up_a, up_b, down_a, down_b, up_2, down_2,
    keep_2, keep_late, keep_early, give,
    item_keep, item_up, item_down, item_up_low, item_down_low, item_relay_up, item_relay_down, sums,
    users, items, uacc, iacc, ugive, igive, eye, in_sem, out_sem,
):
    core = place[3]
    blocks, half, width = keep_2.shape
    near = jnp.where(core == 0, 1, RING - 1)
    far = RING - near
    rows = blocks * half
    h = line_a.shape[0]
    n = 2 * h
    mine, other = core * rows, (1 - core) * rows
    first, rest = [], []
    for k, (piece, at) in enumerate([
            (line_a, 0), (line_b, h), (up_a, n), (up_b, n + h), (down_b, 3 * n), (down_a, 3 * n + h),
            (up_2, 2 * n), (down_2, 2 * n + h)]):
        first.append(pltpu.make_async_copy(piece, items.at[pl.ds(at, piece.shape[0])], in_sem.at[k]))
    moves = [(own, mine, 0, 0), (own, other, 0, half), (ring_2, 0, 2, 0), (over, 0, 2, half),
             (ring, mine, near, 0), (ring, other, near, half),
             (over, rows + 16 + mine, far, 0), (over, rows + 16 + other, far, half)]
    for k, (packet, start, d, at) in enumerate(moves):
        c = pltpu.make_async_copy(
            packet.at[pl.ds(pl.multiple_of(start, 16), rows), :].reshape(blocks, half, width),
            users.at[pl.ds(d * blocks, blocks), pl.ds(at, half), :], in_sem.at[8 + k])
        (first if k < 2 else rest).append(c)
    for c in first + rest:
        c.start()

    uacc[...] = jnp.zeros_like(uacc)
    iacc[...] = jnp.zeros_like(iacc)
    row = lax.broadcasted_iota(jnp.int32, (128, 128), 0)
    col = lax.broadcasted_iota(jnp.int32, (128, 128), 1)
    eye[...] = (row == col).astype(F32)
    for c in first:
        c.wait()

    slope, shift, gain = scalars[0], scalars[1], scalars[2]

    def tile(inner, slope_j, shift_j, label_j):
        y = inner * slope_j + shift_j
        w = pl.reciprocal(1.0 + jnp.exp2(y), approx=True)
        less = 1.0 - w
        near_one = jnp.maximum(w, less)
        low = jnp.minimum(y, 0.0)
        if label_j is not None:
            hit = eye[...] * label_j > 0.5
            ws, lows = [], []
            for q in range(2):
                r = slice(q * 128, (q + 1) * 128)
                keep = slice((1 - q) * 128, (2 - q) * 128)
                wb = jnp.where(hit, -less[r, r], w[r, r])
                lb = jnp.minimum(jnp.where(hit, -y[r, r], y[r, r]), 0.0)
                ws.append(jnp.concatenate([wb, w[r, keep]] if q == 0 else [w[r, keep], wb], axis=1))
                lows.append(jnp.concatenate([lb, low[r, keep]] if q == 0 else [low[r, keep], lb], axis=1))
            w = jnp.concatenate(ws, axis=0)
            low = jnp.concatenate(lows, axis=0)
        scaled = (w * gain).astype(BF)
        nn = near_one.reshape(32, 8, 256)
        logs = jnp.log2(functools.reduce(lambda p, m: p * nn[m], range(1, 32), nn[0]))
        soft_sum = low.reshape(32, 8, 256).sum(0)
        w_sum = w.reshape(32, 8, 256).sum(0)
        return scaled, soft_sum, logs, w_sum

    def one_job(j, carry):
        soft_acc, log_acc, w_acc = carry
        ui, ii, live = jobs[j, 0], jobs[j, 1], jobs[j, 3] == 1
        label_j = jobs[j, 2].astype(F32)
        slope_j = jnp.where(live, slope, 0.0)
        shift_j = jnp.where(live, shift, 1e30)
        it = items[ii]
        u = users[ui]
        inner = lax.dot_general(u, it, NT, preferred_element_type=F32)
        sm, a0, l0, w0 = tile(inner[:half], slope_j, shift_j, label_j)
        so, a1, l1, w1 = tile(inner[half:], slope_j, shift_j, None)
        scaled = jnp.concatenate([sm, so], axis=0)
        uacc[ui] += lax.dot_general(scaled, it, NN, preferred_element_type=F32)
        iacc[ii] += lax.dot_general(scaled, u, TN, preferred_element_type=F32)
        return soft_acc + (a0 + a1), log_acc + (l0 + l1), w_acc + (w0 + w1)

    sends = [
        (ugive, give),
        (iacc.at[pl.ds(n, h)], item_down), (iacc.at[pl.ds(3 * n + h, h)], item_up), (iacc.at[pl.ds(0, n)], item_keep),
        (uacc.at[pl.ds(2 * blocks, blocks), pl.ds(0, half), :], keep_2),
        (uacc.at[pl.ds(far * blocks, blocks), pl.ds(half, half), :], keep_early),
        (uacc.at[pl.ds(far * blocks, blocks), pl.ds(0, half), :], keep_late),
        (igive.at[pl.ds(0, h)], item_relay_down), (igive.at[pl.ds(h, h)], item_relay_up),
        (igive.at[pl.ds(2 * h, h)], item_down_low), (igive.at[pl.ds(3 * h, h)], item_up_low),
    ]
    out = [pltpu.make_async_copy(src, dst, out_sem.at[k]) for k, (src, dst) in enumerate(sends)]

    def lower(d, at, to):
        def one(b, none):
            ugive[to(b)] = uacc[d * blocks + b, pl.ds(at, half), :].astype(BF)
            return none
        lax.fori_loop(0, blocks, one, 0)

    def item_lower(at, to):
        def one(b, none):
            igive[to + b] = iacc[at + b].astype(BF)
            return none
        lax.fori_loop(0, h, one, 0)

    turn = 8
    a_phase = 16 // turn

    def phase(p, carry):
        d = jnp.where(p == 0, 0, jnp.where(p == 1, 2, jnp.where(p == 2, near, far)))

        @pl.when(p == 1)
        def _():
            for c in rest:
                c.wait()

        def some_jobs(g, carry):
            for k in range(turn):
                carry = one_job(d * 16 + turn * g + k, carry)
            return carry

        soft_acc, log_acc, w_acc, scale_acc = carry
        soft_acc, log_acc, w_acc = lax.fori_loop(0, a_phase, some_jobs, (soft_acc, log_acc, w_acc))

        @pl.when(p == 0)
        def _():
            lower(0, 0, lambda b: 3 * blocks + 2 * b + core)
            lower(0, half, lambda b: 3 * blocks + 2 * b + 1 - core)

        @pl.when(p == 1)
        def _():
            lower(2, half, lambda b: b)
            out[4].start()

        @pl.when(p == 2)
        def _():
            lower(near, 0, lambda b: blocks + b)
            lower(near, half, lambda b: 2 * blocks + b)
            out[0].start()

        @pl.when(p == 3)
        def _():
            item_lower(2 * n, 0)
            out[7].start()
            item_lower(2 * n + h, h)
            out[8].start()
            for k in (1, 2, 3, 5, 6):
                out[k].start()
            item_lower(n + h, 2 * h)
            out[9].start()
            item_lower(3 * n, 3 * h)
            out[10].start()

        def scale_sum(b, acc):
            prod = uacc[d * blocks + b] * users[d * blocks + b].astype(F32)
            return acc + prod.reshape(64, 8, 256).sum(0)

        return soft_acc, log_acc, w_acc, lax.fori_loop(0, blocks, scale_sum, scale_acc)

    zero = jnp.zeros((8, 256), F32)
    soft_acc, log_acc, w_acc, scale_acc = lax.fori_loop(0, RING, phase, (zero, zero, zero, zero))

    total = [(soft_acc + log_acc) * (-1.0 / LOG2E), scale_acc * scalars[3], w_acc]
    lane = lax.broadcasted_iota(jnp.int32, (8, 256), 1)
    packed = jnp.zeros((8, 256), F32)
    for k in range(3):
        packed = jnp.where(lane == k, jnp.sum(total[k]), packed)
    packed = jnp.where(lane == 3, 0.5 * jobs[0, 4].astype(F32), packed)
    sums[...] = packed
    for c in out:
        c.wait()


def score(place, jobs, scalars, pieces):
    n, half, width = pieces[4].shape
    n = 2 * n
    blocks = 4
    height = 2 * half
    n_users, n_items = RING * blocks, RING * n
    smem = pl.BlockSpec(memory_space=pltpu.SMEM)
    any_ = pl.BlockSpec(memory_space=pl.ANY)
    part = (blocks, half, width)
    return pl.pallas_call(
        score_kernel,
        in_specs=[smem, smem, smem] + [any_] * len(pieces),
        out_specs=[any_] * 11 + [pl.BlockSpec(memory_space=pltpu.VMEM)],
        out_shape=[jax.ShapeDtypeStruct(part, F32)] * 3 + [jax.ShapeDtypeStruct((5 * blocks, half, width), BF)]
        + [jax.ShapeDtypeStruct((n, half, width), F32)] + [jax.ShapeDtypeStruct((n // 2, half, width), F32)] * 2
        + [jax.ShapeDtypeStruct((n // 2, half, width), BF)] * 4
        + [jax.ShapeDtypeStruct((8, width), F32)],
        scratch_shapes=[
            pltpu.VMEM((n_users, height, width), BF),
            pltpu.VMEM((n_items, half, width), BF),
            pltpu.VMEM((n_users, height, width), F32),
            pltpu.VMEM((n_items, half, width), F32),
            pltpu.VMEM((5 * blocks, half, width), BF),
            pltpu.VMEM((2 * n, half, width), BF),
            pltpu.VMEM((128, 128), F32),
            pltpu.SemaphoreType.DMA((16,)),
            pltpu.SemaphoreType.DMA((16,)),
        ],
        compiler_params=pltpu.CompilerParams(vmem_limit_bytes=36 * 2**20),
        cost_estimate=pl.CostEstimate(flops=13 * 10**9, bytes_accessed=20 * 2**20, transcendentals=2 * 10**7),
    )(place, jobs, scalars, *pieces)


def finish_kernel(place, give, given, early, late, early_over, late_over, out):
    first = place[3] == 0
    half = early.shape[1]
    for k, (ours, theirs) in enumerate([((late, early_over), (late_over, early)), ((early, late_over), (early_over, late))]):
        a = jnp.where(first, ours[0][0].astype(F32), theirs[0][0].astype(F32))
        b = jnp.where(first, ours[1][0].astype(F32), theirs[1][0].astype(F32))
        own = give[k].astype(F32) + given[k].astype(F32)
        out[0, k * half: (k + 1) * half, :] = own + (a + b)


def finish(place, give, given, early, late, early_over, late_over):
    blocks, half, width = early.shape
    own = pl.BlockSpec((2, half, width), lambda b: (3 * blocks // 2 + b, 0, 0))
    part = pl.BlockSpec((1, half, width), lambda b: (b, 0, 0))
    return pl.pallas_call(
        finish_kernel,
        grid=(blocks,),
        in_specs=[pl.BlockSpec(memory_space=pltpu.SMEM), own, own, part, part, part, part],
        out_specs=pl.BlockSpec((1, 2 * half, width), lambda b: (b, 0, 0)),
        out_shape=jax.ShapeDtypeStruct((blocks, 2 * half, width), F32),
        compiler_params=pltpu.CompilerParams(vmem_limit_bytes=8 * 2**20),
        cost_estimate=pl.CostEstimate(flops=2 * 10**6, bytes_accessed=6 * 2**20, transcendentals=0),
    )(place, give, given, early, late, early_over, late_over)


def device(x, y, z, core):
    return (((x % RING) * RING + y % RING) * RING + z % RING) * 2 + core


def every():
    return [(x, y, z, c) for x in range(RING) for y in range(RING) for z in range(RING) for c in range(2)]


AXES = ("x", "y", "z", "n")


def named(f):
    def call(a, *rest, name):
        with jax.named_scope(name):
            return f(a, *rest)
    return call


@named
def along_z(a):
    return lax.ppermute(a, AXES, [
        (device(x, y, z, c), device(x, y, z + (-1 if c else 1), c)) for x, y, z, c in every()])


@named
def swap(a, bit):
    return lax.ppermute(a, AXES, [(i, i ^ bit) for i in range(128)])


@named
def along_first(a, d):
    return lax.ppermute(a, AXES, [
        (device(x, y, z, c), device(x + (d if c else 0), y + (0 if c else d), z, c)) for x, y, z, c in every()])


@named
def along_second(a, d):
    return lax.ppermute(a, AXES, [
        (device(x, y, z, c), device(x + (0 if c else d), y + (d if c else 0), z, c)) for x, y, z, c in every()])


@named
def across(a):
    return lax.ppermute(a, AXES, [(device(x, y, z, c), device(x, y, z, 1 - c)) for x, y, z, c in every()])


def body(user_emb, item_emb, pairs, counts, natural_exponent_param, additive_shift_param):
    my_x, my_y, my_z = lax.axis_index("x"), lax.axis_index("y"), lax.axis_index("z")
    core = lax.axis_index("n")
    blocks, height, width = user_emb.shape
    half = height // 2
    sharpness = jnp.exp(natural_exponent_param[0])
    shift = additive_shift_param[0]
    place = jnp.stack([my_x, my_y, my_z, core]).astype(jnp.int32)
    scalars = jnp.stack([-sharpness * LOG2E, -shift * LOG2E, sharpness * height ** -0.5, jnp.float32(height ** 0.5)])

    slots = pairs.shape[1]
    rows = jnp.concatenate([pairs[0].T, jnp.broadcast_to(counts[:, None], (1, slots))], axis=0)
    rows = jnp.pad(rows.astype(F32), ((0, 12), (0, width - slots))).astype(BF)
    lower = [user_emb[:, :half].astype(BF).reshape(blocks * half, width),
             user_emb[:, half:].astype(BF).reshape(blocks * half, width)]
    own = jnp.concatenate(lower + [rows], axis=0)
    items_low = item_emb.astype(BF)

    line = [items_low] + [along_first(items_low, d, name="items_line") for d in (1, 2, 3)]
    line_a, line_b = jnp.concatenate(line[:2], axis=0), jnp.concatenate(line[2:], axis=0)
    h = line_a.shape[0]
    up_a, down_a = along_second(line_a, 1, name="items_up_a"), along_second(line_b, -1, name="items_down_a")
    up_b, down_b = along_second(line_b, 1, name="items_up_b"), along_second(line_a, -1, name="items_down_b")
    up_2, down_2 = along_second(up_a, 1, name="items_up_2"), along_second(down_a, -1, name="items_down_2")
    ring = along_z(own, name="users_ring")
    n_rows = blocks * half
    mine = lax.dynamic_slice_in_dim(ring, core * n_rows, n_rows, axis=0)
    ring_2 = along_z(jnp.concatenate([mine, ring[2 * n_rows:]], axis=0), name="users_ring_2")
    lists = ring_2[n_rows:] + (up_a[0, :16] + down_a[0, :16] + up_b[0, :16] + down_b[0, :16]) * 0
    over = across(jnp.concatenate([ring_2[:n_rows], lists, ring], axis=0), name="users_over")

    jobs = plan(place, own, ring, ring_2, over, up_b, down_b)
    (keep_2, keep_late, keep_early, give,
     item_keep, item_up, item_down, item_up_low, item_down_low, item_relay_up, item_relay_down, sums) = score(
        place, jobs, scalars, [own, ring, ring_2, over, line_a, line_b, up_a, up_b, down_a, down_b, up_2, down_2])

    given = across(give, name="give")

    steps = []
    for k in range(7):
        if k == 3:
            sums = sums + given[0, :8].astype(F32) * 0.0
        sums = sums + swap(sums, 1 << k, name="totals_" + str(k))
        steps.append(sums)
    objective = sums[0, :3] / (height * height * sums[0, 3])

    def after(step, a):
        return (a.reshape(-1, 8, width) + steps[step - 1] * 0.0).reshape(a.shape)

    from_up = along_second(item_relay_down, -1, name="item_relay_down")
    from_down = along_second(item_relay_up, 1, name="item_relay_up")
    item_down = jnp.concatenate([after(3, item_down + from_up.astype(F32)).astype(BF), item_down_low])
    item_up = jnp.concatenate([item_up_low, after(3, item_up + from_down.astype(F32)).astype(BF)])
    item_down = along_second(item_down, -1, name="item_down")
    item_up = along_second(item_up, 1, name="item_up")
    item_line = after(5, item_keep + item_down.astype(F32) + item_up.astype(F32))
    back = [along_first(item_line[2 * d: 2 * d + 2].astype(BF), -d, name="item_back") for d in (1, 2, 3)]
    item_grad = item_line[:2] + back[0].astype(F32) + back[1].astype(F32) + back[2].astype(F32)

    relay = along_z((keep_2 + given[:blocks].astype(F32)).astype(BF), name="user_relay")
    early = along_z((keep_early + given[blocks:2 * blocks].astype(F32)).astype(BF), name="user_early")
    late = along_z((keep_late + early[0, :1].astype(F32) * 0.0 + given[2 * blocks:3 * blocks].astype(F32) + relay.astype(F32)).astype(BF), name="user_late")
    early_over, late_over = across(early, name="early_over"), across(late, name="late_over")
    user_grad = finish(place, give, given, early, late, early_over, late_over)
    return user_grad, item_grad, objective


def solution(mesh):
    grid = Mesh(mesh.devices.reshape(RING, RING, RING, 2), AXES)
    return jax.shard_map(
        body,
        mesh=grid,
        in_specs=(P(WIDE, None, None), P(WIDE, "n", None), P(WIDE, None, None), P(WIDE), P(), P()),
        out_specs=(P(WIDE, None, None), P(WIDE, "n", None), P()),
        check_vma=False,
    )
```

```python
import functools

import jax
import jax.numpy as jnp
from jax import lax
from jax.experimental import pallas as pl
from jax.experimental.pallas import tpu as pltpu
from jax.sharding import Mesh
from jax.sharding import PartitionSpec as P

LOG2E = 1.4426950408889634
RING = 4
NT = (((1,), (1,)), ((), ()))
NN = (((1,), (0,)), ((), ()))
TN = (((0,), (0,)), ((), ()))
WIDE = ("x", "y", "z")
BF = jnp.bfloat16
F32 = jnp.float32


def plan_kernel(place, own, ring, ring_2, over, *rest):
    jobs, rows_low, sem = rest[-3:]
    my_x, my_y, my_z, core = place[0], place[1], place[2], place[3]
    near = jnp.where(core == 0, 1, RING - 1)
    copies = []
    for k, (packet, d) in enumerate([(own, 0), (ring, near), (over, RING - near), (ring_2, 2)]):
        to = rows_low.at[pl.ds(pl.multiple_of(d * 16, 16), 16), :]
        copies.append(pltpu.make_async_copy(packet.at[pl.ds(packet.shape[0] - 16, 16), :], to, sem.at[k]))
    for c in copies:
        c.start()
    for c in copies:
        c.wait()
    width = rows_low.shape[1]
    owner_id = lax.broadcasted_iota(jnp.int32, (16, width), 0)
    slot = lax.broadcasted_iota(jnp.int32, (16, width), 1)
    lane = lax.broadcasted_iota(jnp.int32, (16, 128), 1)
    for d in range(RING):
        rows = rows_low[16 * d: 16 * d + 16, :].astype(F32)
        user, item, label = (jnp.broadcast_to(rows[k: k + 1], (16, width)) for k in range(3))
        live_slots = jnp.broadcast_to(rows[3:4, :1], (16, width))
        item = item.astype(jnp.int32)
        mine = (((item >> 1) & 3) == my_z) & ((item >> 3) == owner_id) & (slot.astype(F32) < live_slots)
        dx = (my_x - (item >> 5)) & 3
        dy = (my_y - ((item >> 3) & 3)) & 3
        at = jnp.where(core == 0, dx * 4 + dy, dy * 4 + dx) * 2 + (item & 1)
        block = d * 4 + (user.astype(jnp.int32) & 3)
        out = jnp.zeros((16, 128), F32)
        for k, v in enumerate([block.astype(F32), at.astype(F32), label, jnp.ones_like(label)]):
            out = jnp.where(lane == k, jnp.sum(jnp.where(mine, v, 0.0), axis=1, keepdims=True), out)
        if d == 0:
            out = jnp.where(lane == 4, live_slots[:, :128], out)
        jobs[16 * d: 16 * d + 16, :] = out.astype(jnp.int32)


def plan(place, own, ring, ring_2, over, *before):
    hbm = pl.BlockSpec(memory_space=pl.ANY)
    width = own.shape[1]
    return pl.pallas_call(
        plan_kernel,
        in_specs=[pl.BlockSpec(memory_space=pltpu.SMEM)] + [hbm] * (4 + len(before)),
        out_specs=pl.BlockSpec(memory_space=pltpu.VMEM),
        out_shape=jax.ShapeDtypeStruct((64, 128), jnp.int32),
        scratch_shapes=[pltpu.VMEM((64, width), BF), pltpu.SemaphoreType.DMA((4,))],
        compiler_params=pltpu.CompilerParams(vmem_limit_bytes=2**20),
        cost_estimate=pl.CostEstimate(flops=10**6, bytes_accessed=2**20, transcendentals=0),
    )(place, own, ring, ring_2, over, *before)


def score_kernel(
    place, jobs, scalars, own, ring, ring_2, over, line_a, line_b, up_a, up_b, down_a, down_b, up_2, down_2,
    keep_2, keep_late, keep_early, give,
    item_keep, item_up, item_down, item_up_low, item_down_low, item_relay_up, item_relay_down, sums,
    users, items, uacc, iacc, ugive, igive, eye, in_sem, out_sem,
):
    core = place[3]
    blocks, half, width = keep_2.shape
    near = jnp.where(core == 0, 1, RING - 1)
    far = RING - near
    rows = blocks * half
    h = line_a.shape[0]
    n = 2 * h
    mine, other = core * rows, (1 - core) * rows
    first, rest = [], []
    for k, (piece, at) in enumerate([
            (line_a, 0), (line_b, h), (up_a, n), (up_b, n + h), (down_b, 3 * n), (down_a, 3 * n + h),
            (up_2, 2 * n), (down_2, 2 * n + h)]):
        first.append(pltpu.make_async_copy(piece, items.at[pl.ds(at, piece.shape[0])], in_sem.at[k]))
    moves = [(own, mine, 0, 0), (own, other, 0, half), (ring_2, 0, 2, 0), (over, 0, 2, half),
             (ring, mine, near, 0), (ring, other, near, half),
             (over, rows + 16 + mine, far, 0), (over, rows + 16 + other, far, half)]
    for k, (packet, start, d, at) in enumerate(moves):
        c = pltpu.make_async_copy(
            packet.at[pl.ds(pl.multiple_of(start, 16), rows), :].reshape(blocks, half, width),
            users.at[pl.ds(d * blocks, blocks), pl.ds(at, half), :], in_sem.at[8 + k])
        (first if k < 2 else rest).append(c)
    for c in first + rest:
        c.start()

    uacc[...] = jnp.zeros_like(uacc)
    iacc[...] = jnp.zeros_like(iacc)
    row = lax.broadcasted_iota(jnp.int32, (128, 128), 0)
    col = lax.broadcasted_iota(jnp.int32, (128, 128), 1)
    eye[...] = (row == col).astype(F32)
    for c in first:
        c.wait()

    slope, shift, gain = scalars[0], scalars[1], scalars[2]

    def tile(inner, slope_j, shift_j, label_j):
        y = inner * slope_j + shift_j
        w = pl.reciprocal(1.0 + jnp.exp2(y), approx=True)
        less = 1.0 - w
        near_one = jnp.maximum(w, less)
        low = jnp.minimum(y, 0.0)
        if label_j is not None:
            hit = eye[...] * label_j > 0.5
            ws, lows = [], []
            for q in range(2):
                r = slice(q * 128, (q + 1) * 128)
                keep = slice((1 - q) * 128, (2 - q) * 128)
                wb = jnp.where(hit, -less[r, r], w[r, r])
                lb = jnp.minimum(jnp.where(hit, -y[r, r], y[r, r]), 0.0)
                ws.append(jnp.concatenate([wb, w[r, keep]] if q == 0 else [w[r, keep], wb], axis=1))
                lows.append(jnp.concatenate([lb, low[r, keep]] if q == 0 else [low[r, keep], lb], axis=1))
            w = jnp.concatenate(ws, axis=0)
            low = jnp.concatenate(lows, axis=0)
        scaled = (w * gain).astype(BF)
        nn = near_one.reshape(32, 8, 256)
        logs = jnp.log2(functools.reduce(lambda p, m: p * nn[m], range(1, 32), nn[0]))
        soft_sum = low.reshape(32, 8, 256).sum(0)
        w_sum = w.reshape(32, 8, 256).sum(0)
        return scaled, soft_sum, logs, w_sum

    def one_job(j, carry):
        soft_acc, log_acc, w_acc = carry
        ui, ii, live = jobs[j, 0], jobs[j, 1], jobs[j, 3] == 1
        label_j = jobs[j, 2].astype(F32)
        slope_j = jnp.where(live, slope, 0.0)
        shift_j = jnp.where(live, shift, 1e30)
        it = items[ii]
        u = users[ui]
        inner = lax.dot_general(u, it, NT, preferred_element_type=F32)
        sm, a0, l0, w0 = tile(inner[:half], slope_j, shift_j, label_j)
        so, a1, l1, w1 = tile(inner[half:], slope_j, shift_j, None)
        scaled = jnp.concatenate([sm, so], axis=0)
        uacc[ui] += lax.dot_general(scaled, it, NN, preferred_element_type=F32)
        iacc[ii] += lax.dot_general(scaled, u, TN, preferred_element_type=F32)
        return soft_acc + (a0 + a1), log_acc + (l0 + l1), w_acc + (w0 + w1)

    sends = [
        (ugive, give),
        (iacc.at[pl.ds(n, h)], item_down), (iacc.at[pl.ds(3 * n + h, h)], item_up), (iacc.at[pl.ds(0, n)], item_keep),
        (uacc.at[pl.ds(2 * blocks, blocks), pl.ds(0, half), :], keep_2),
        (uacc.at[pl.ds(far * blocks, blocks), pl.ds(half, half), :], keep_early),
        (uacc.at[pl.ds(far * blocks, blocks), pl.ds(0, half), :], keep_late),
        (igive.at[pl.ds(0, h)], item_relay_down), (igive.at[pl.ds(h, h)], item_relay_up),
        (igive.at[pl.ds(2 * h, h)], item_down_low), (igive.at[pl.ds(3 * h, h)], item_up_low),
    ]
    out = [pltpu.make_async_copy(src, dst, out_sem.at[k]) for k, (src, dst) in enumerate(sends)]

    def lower(d, at, to):
        def one(b, none):
            ugive[to(b)] = uacc[d * blocks + b, pl.ds(at, half), :].astype(BF)
            return none
        lax.fori_loop(0, blocks, one, 0)

    def item_lower(at, to):
        def one(b, none):
            igive[to + b] = iacc[at + b].astype(BF)
            return none
        lax.fori_loop(0, h, one, 0)

    turn = 16
    a_phase = 16 // turn

    def phase(p, carry):
        d = jnp.where(p == 0, 0, jnp.where(p == 1, 2, jnp.where(p == 2, near, far)))

        @pl.when(p == 1)
        def _():
            for c in rest:
                c.wait()

        def some_jobs(g, carry):
            for k in range(turn):
                carry = one_job(d * 16 + turn * g + k, carry)
            return carry

        soft_acc, log_acc, w_acc, scale_acc = carry
        soft_acc, log_acc, w_acc = lax.fori_loop(0, a_phase, some_jobs, (soft_acc, log_acc, w_acc))

        @pl.when(p == 0)
        def _():
            lower(0, 0, lambda b: 3 * blocks + 2 * b + core)
            lower(0, half, lambda b: 3 * blocks + 2 * b + 1 - core)

        @pl.when(p == 1)
        def _():
            lower(2, half, lambda b: b)
            out[4].start()

        @pl.when(p == 2)
        def _():
            lower(near, 0, lambda b: blocks + b)
            lower(near, half, lambda b: 2 * blocks + b)
            out[0].start()

        @pl.when(p == 3)
        def _():
            for k in (1, 2, 3, 5, 6):
                out[k].start()
            item_lower(2 * n, 0)
            out[7].start()
            item_lower(2 * n + h, h)
            out[8].start()
            item_lower(n + h, 2 * h)
            out[9].start()
            item_lower(3 * n, 3 * h)
            out[10].start()

        def scale_sum(b, acc):
            prod = uacc[d * blocks + b] * users[d * blocks + b].astype(F32)
            return acc + prod.reshape(64, 8, 256).sum(0)

        return soft_acc, log_acc, w_acc, lax.fori_loop(0, blocks, scale_sum, scale_acc)

    zero = jnp.zeros((8, 256), F32)
    soft_acc, log_acc, w_acc, scale_acc = lax.fori_loop(0, RING, phase, (zero, zero, zero, zero))

    total = [(soft_acc + log_acc) * (-1.0 / LOG2E), scale_acc * scalars[3], w_acc]
    lane = lax.broadcasted_iota(jnp.int32, (8, 256), 1)
    packed = jnp.zeros((8, 256), F32)
    for k in range(3):
        packed = jnp.where(lane == k, jnp.sum(total[k]), packed)
    packed = jnp.where(lane == 3, 0.5 * jobs[0, 4].astype(F32), packed)
    sums[...] = packed
    for c in out:
        c.wait()


def score(place, jobs, scalars, pieces):
    n, half, width = pieces[4].shape
    n = 2 * n
    blocks = 4
    height = 2 * half
    n_users, n_items = RING * blocks, RING * n
    smem = pl.BlockSpec(memory_space=pltpu.SMEM)
    any_ = pl.BlockSpec(memory_space=pl.ANY)
    part = (blocks, half, width)
    return pl.pallas_call(
        score_kernel,
        in_specs=[smem, smem, smem] + [any_] * len(pieces),
        out_specs=[any_] * 11 + [pl.BlockSpec(memory_space=pltpu.VMEM)],
        out_shape=[jax.ShapeDtypeStruct(part, F32)] * 3 + [jax.ShapeDtypeStruct((5 * blocks, half, width), BF)]
        + [jax.ShapeDtypeStruct((n, half, width), F32)] + [jax.ShapeDtypeStruct((n // 2, half, width), F32)] * 2
        + [jax.ShapeDtypeStruct((n // 2, half, width), BF)] * 4
        + [jax.ShapeDtypeStruct((8, width), F32)],
        scratch_shapes=[
            pltpu.VMEM((n_users, height, width), BF),
            pltpu.VMEM((n_items, half, width), BF),
            pltpu.VMEM((n_users, height, width), F32),
            pltpu.VMEM((n_items, half, width), F32),
            pltpu.VMEM((5 * blocks, half, width), BF),
            pltpu.VMEM((2 * n, half, width), BF),
            pltpu.VMEM((128, 128), F32),
            pltpu.SemaphoreType.DMA((16,)),
            pltpu.SemaphoreType.DMA((16,)),
        ],
        compiler_params=pltpu.CompilerParams(vmem_limit_bytes=36 * 2**20),
        cost_estimate=pl.CostEstimate(flops=13 * 10**9, bytes_accessed=20 * 2**20, transcendentals=2 * 10**7),
    )(place, jobs, scalars, *pieces)


def finish_kernel(place, give, given, early, late, early_over, late_over, out):
    first = place[3] == 0
    half = early.shape[1]
    for k, (ours, theirs) in enumerate([((late, early_over), (late_over, early)), ((early, late_over), (early_over, late))]):
        a = jnp.where(first, ours[0][0].astype(F32), theirs[0][0].astype(F32))
        b = jnp.where(first, ours[1][0].astype(F32), theirs[1][0].astype(F32))
        own = give[k].astype(F32) + given[k].astype(F32)
        out[0, k * half: (k + 1) * half, :] = own + (a + b)


def finish(place, give, given, early, late, early_over, late_over):
    blocks, half, width = early.shape
    own = pl.BlockSpec((2, half, width), lambda b: (3 * blocks // 2 + b, 0, 0))
    part = pl.BlockSpec((1, half, width), lambda b: (b, 0, 0))
    return pl.pallas_call(
        finish_kernel,
        grid=(blocks,),
        in_specs=[pl.BlockSpec(memory_space=pltpu.SMEM), own, own, part, part, part, part],
        out_specs=pl.BlockSpec((1, 2 * half, width), lambda b: (b, 0, 0)),
        out_shape=jax.ShapeDtypeStruct((blocks, 2 * half, width), F32),
        compiler_params=pltpu.CompilerParams(vmem_limit_bytes=8 * 2**20),
        cost_estimate=pl.CostEstimate(flops=2 * 10**6, bytes_accessed=6 * 2**20, transcendentals=0),
    )(place, give, given, early, late, early_over, late_over)


def device(x, y, z, core):
    return (((x % RING) * RING + y % RING) * RING + z % RING) * 2 + core


def every():
    return [(x, y, z, c) for x in range(RING) for y in range(RING) for z in range(RING) for c in range(2)]


AXES = ("x", "y", "z", "n")


def named(f):
    def call(a, *rest, name):
        with jax.named_scope(name):
            return f(a, *rest)
    return call


@named
def along_z(a):
    return lax.ppermute(a, AXES, [
        (device(x, y, z, c), device(x, y, z + (-1 if c else 1), c)) for x, y, z, c in every()])


@named
def swap(a, bit):
    return lax.ppermute(a, AXES, [(i, i ^ bit) for i in range(128)])


@named
def along_first(a, d):
    return lax.ppermute(a, AXES, [
        (device(x, y, z, c), device(x + (d if c else 0), y + (0 if c else d), z, c)) for x, y, z, c in every()])


@named
def along_second(a, d):
    return lax.ppermute(a, AXES, [
        (device(x, y, z, c), device(x + (0 if c else d), y + (d if c else 0), z, c)) for x, y, z, c in every()])


@named
def across(a):
    return lax.ppermute(a, AXES, [(device(x, y, z, c), device(x, y, z, 1 - c)) for x, y, z, c in every()])


def body(user_emb, item_emb, pairs, counts, natural_exponent_param, additive_shift_param):
    my_x, my_y, my_z = lax.axis_index("x"), lax.axis_index("y"), lax.axis_index("z")
    core = lax.axis_index("n")
    blocks, height, width = user_emb.shape
    half = height // 2
    sharpness = jnp.exp(natural_exponent_param[0])
    shift = additive_shift_param[0]
    place = jnp.stack([my_x, my_y, my_z, core]).astype(jnp.int32)
    scalars = jnp.stack([-sharpness * LOG2E, -shift * LOG2E, sharpness * height ** -0.5, jnp.float32(height ** 0.5)])

    slots = pairs.shape[1]
    rows = jnp.concatenate([pairs[0].T, jnp.broadcast_to(counts[:, None], (1, slots))], axis=0)
    rows = jnp.pad(rows.astype(F32), ((0, 12), (0, width - slots))).astype(BF)
    lower = [user_emb[:, :half].astype(BF).reshape(blocks * half, width),
             user_emb[:, half:].astype(BF).reshape(blocks * half, width)]
    own = jnp.concatenate(lower + [rows], axis=0)
    items_low = item_emb.astype(BF)

    line = [items_low] + [along_first(items_low, d, name="items_line") for d in (1, 2, 3)]
    line_a, line_b = jnp.concatenate(line[:2], axis=0), jnp.concatenate(line[2:], axis=0)
    h = line_a.shape[0]
    up_a, down_a = along_second(line_a, 1, name="items_up_a"), along_second(line_b, -1, name="items_down_a")
    up_b, down_b = along_second(line_b, 1, name="items_up_b"), along_second(line_a, -1, name="items_down_b")
    up_2, down_2 = along_second(up_a, 1, name="items_up_2"), along_second(down_a, -1, name="items_down_2")
    ring = along_z(own, name="users_ring")
    n_rows = blocks * half
    mine = lax.dynamic_slice_in_dim(ring, core * n_rows, n_rows, axis=0)
    ring_2 = along_z(jnp.concatenate([mine, ring[2 * n_rows:]], axis=0), name="users_ring_2")
    lists = ring_2[n_rows:] + (up_a[0, :16] + down_a[0, :16] + up_b[0, :16] + down_b[0, :16]) * 0
    over = across(jnp.concatenate([ring_2[:n_rows], lists, ring], axis=0), name="users_over")

    jobs = plan(place, own, ring, ring_2, over, up_b, down_b)
    (keep_2, keep_late, keep_early, give,
     item_keep, item_up, item_down, item_up_low, item_down_low, item_relay_up, item_relay_down, sums) = score(
        place, jobs, scalars, [own, ring, ring_2, over, line_a, line_b, up_a, up_b, down_a, down_b, up_2, down_2])

    given = across(give, name="give")

    steps = []
    for k in range(7):
        if k == 3:
            sums = sums + given[0, :8].astype(F32) * 0.0
        sums = sums + swap(sums, 1 << k, name="totals_" + str(k))
        steps.append(sums)
    objective = sums[0, :3] / (height * height * sums[0, 3])

    def after(step, a):
        return (a.reshape(-1, 8, width) + steps[step - 1] * 0.0).reshape(a.shape)

    from_up = along_second(item_relay_down, -1, name="item_relay_down")
    from_down = along_second(item_relay_up, 1, name="item_relay_up")
    item_down = jnp.concatenate([after(3, item_down + from_up.astype(F32)).astype(BF), item_down_low])
    item_up = jnp.concatenate([item_up_low, after(3, item_up + from_down.astype(F32)).astype(BF)])
    item_down = along_second(item_down, -1, name="item_down")
    item_up = along_second(item_up, 1, name="item_up")
    item_line = after(5, item_keep + item_down.astype(F32) + item_up.astype(F32))
    back = [along_first(item_line[2 * d: 2 * d + 2].astype(BF), -d, name="item_back") for d in (1, 2, 3)]
    item_grad = item_line[:2] + back[0].astype(F32) + back[1].astype(F32) + back[2].astype(F32)

    relay = along_z((keep_2 + given[:blocks].astype(F32)).astype(BF), name="user_relay")
    early = along_z((keep_early + given[blocks:2 * blocks].astype(F32)).astype(BF), name="user_early")
    late = along_z((keep_late + early[0, :1].astype(F32) * 0.0 + given[2 * blocks:3 * blocks].astype(F32) + relay.astype(F32)).astype(BF), name="user_late")
    early_over, late_over = across(early, name="early_over"), across(late, name="late_over")
    user_grad = finish(place, give, given, early, late, early_over, late_over)
    return user_grad, item_grad, objective


def solution(mesh):
    grid = Mesh(mesh.devices.reshape(RING, RING, RING, 2), AXES)
    return jax.shard_map(
        body,
        mesh=grid,
        in_specs=(P(WIDE, None, None), P(WIDE, "n", None), P(WIDE, None, None), P(WIDE), P(), P()),
        out_specs=(P(WIDE, None, None), P(WIDE, "n", None), P()),
        check_vma=False,
    )
```
